256 devices in a mesh: tm: 64 (over x, z, core), chan: 4 (over y).
Axes of the slice: x: 4, y: 4, z: 8, core: 2. Of those that a mesh axis runs over, the one named last changes fastest.
Arguments:
- features: bfloat16 [393216, 512], P('tm', 'chan'), may hold values from -6 to 6
- snake_alpha: float32 [512], P('chan'), may hold values from 0.5 to 3
- down_weight: bfloat16 [512, 16, 1024], P(None, None, 'chan'), may hold values from -0.0625 to 0.0625
- grad_out: bfloat16 [49152, 1024], P('tm', 'chan'), may hold values from -6 to 6
Outputs:
- encoded: bfloat16 [49152, 1024], P('tm', 'chan')
- grad_features: bfloat16 [393216, 512], P('tm', 'chan')
- grad_down: bfloat16 [1024, 16, 512], P('tm', None, 'chan')
The draws below stay inside these ranges and needn't reach their ends.
All inputs are finite; a program needn't handle non-finite values.
Results may differ from the reference program's by a relative error of at most 0.0049.
Values may be sent and summed in bfloat16 or wider, within the bound.
No kernel may reach another device: no remote copies, remote signals or barrier semaphores. Data moves between devices by JAX's collectives and lax.ppermute only.
A program may use at most 128 MiB of HBM per device.

```python
import math
import jax
import jax.numpy as jnp

C = 512
OUTC = 1024
STRIDE = 8
FRAMES = 393216
OUT_FRAMES = 49152


def level_of(own_key, extent, pieces, least, high):
    level, own = 1.0, jax.random.fold_in(own_key, 6)
    for axis_at, parts in pieces:
        heights = jnp.exp(jax.random.uniform(jax.random.fold_in(own, axis_at), (parts,), jnp.float32, least / len(pieces), high / len(pieces)))
        level = level * jnp.repeat(heights, extent[axis_at] // parts).reshape([-1 if axis == axis_at else 1 for axis in range(len(extent))])
    return level


def centred(key, dims, scale, bound, split=(), kind=jnp.bfloat16):
    level = level_of(key, dims, split, -0.22, 0.18) if split else 1.0
    array = jax.random.normal(key, dims, jnp.float32) * scale * level
    return jnp.minimum(jnp.maximum(array, -bound), bound).astype(kind)


def setup_inputs(seed: int = 0) -> dict:
    streams_of = jax.random.split(jax.random.key(seed), 5)
    features = centred(streams_of[0], (FRAMES, C), 1.0, 6.0, ((0, 64), (1, 4)))
    snake_alpha = jnp.clip(jnp.exp(math.log(3.0) - 1.7917595 * jax.random.uniform(streams_of[1], (C,), jnp.float32) ** level_of(streams_of[1], (C,), ((0, 4),), -0.2, 0.2)), 0.5, 3.0)
    down_weight = centred(streams_of[2], (C, 2 * STRIDE, OUTC), (2 * STRIDE * C) ** -0.5, 0.0625, ((2, 4),))
    grad_out = centred(streams_of[3], (OUT_FRAMES, OUTC), 1.0, 6.0, ((0, 64), (1, 4)))
    return dict(features=features, snake_alpha=snake_alpha, down_weight=down_weight, grad_out=grad_out)


def snake(values, alpha):
    return values + jnp.sin(alpha * values) ** 2 / alpha

def reference(features, snake_alpha, down_weight, grad_out):
    wide = features.astype(jnp.float32)
    snaked = snake(wide, snake_alpha).astype(jnp.bfloat16)
    half = STRIDE // 2
    padded = jnp.pad(snaked, ((half, half), (0, 0)))
    tiled = padded.reshape(OUT_FRAMES + 1, STRIDE * C)
    early = jnp.transpose(down_weight[:, :STRIDE], (1, 0, 2)).reshape(STRIDE * C, OUTC)
    late = jnp.transpose(down_weight[:, STRIDE:], (1, 0, 2)).reshape(STRIDE * C, OUTC)
    encoded = (jnp.dot(tiled[:-1], early, preferred_element_type=jnp.float32) + jnp.dot(tiled[1:], late, preferred_element_type=jnp.float32)).astype(jnp.bfloat16)
    grad_pad = jnp.pad(grad_out, ((1, 1), (0, 0)))
    spread = jnp.dot(grad_pad[1:], early.T, preferred_element_type=jnp.float32) + jnp.dot(grad_pad[:-1], late.T, preferred_element_type=jnp.float32)
    grad_snaked = spread.reshape(FRAMES + STRIDE, C)[half:half + FRAMES]
    grad_features = (grad_snaked * (1.0 + jnp.sin(2.0 * snake_alpha * wide))).astype(jnp.bfloat16)
    lower = jnp.dot(tiled[:-1].T, grad_out, preferred_element_type=jnp.float32)
    upper = jnp.dot(tiled[1:].T, grad_out, preferred_element_type=jnp.float32)
    lower = jnp.transpose(lower.reshape(STRIDE, C, OUTC), (2, 0, 1))
    upper = jnp.transpose(upper.reshape(STRIDE, C, OUTC), (2, 0, 1))
    scale = 1.0 / math.sqrt(OUT_FRAMES)
    grad_down = (jnp.concatenate([lower, upper], axis=1) * scale).astype(jnp.bfloat16)
    return (encoded, grad_features, grad_down)
```

```python
import functools
import math

import jax
import jax.numpy as jnp
from jax import lax
from jax.experimental import pallas as pl
from jax.experimental.pallas import tpu as pltpu
from jax.sharding import Mesh
from jax.sharding import PartitionSpec as P

STRIDE = 8
TAPS = 16
BF = jnp.bfloat16
F32 = jnp.float32
TM = ("x", "z", "core")
SIN = (1.0, -1.66666666e-01, 8.33333079e-03, -1.98408371e-04, 2.75240247e-06, -2.38669497e-08)
COS = (
    1.0,
    -0.5,
    4.16666665e-02,
    -1.38888838e-03,
    2.48010074e-05,
    -2.75233926e-07,
    1.98888297e-09,
)
PI_A = 3.140625
PI_B = math.pi - PI_A
VMEM = pl.BlockSpec(memory_space=pltpu.VMEM)
SMEM = pl.BlockSpec(memory_space=pltpu.SMEM)
ANY = pl.BlockSpec(memory_space=pl.ANY)
LIMIT = 56 * 2**20


def params():
    return pltpu.CompilerParams(vmem_limit_bytes=LIMIT)


def cost(flops, moved):
    return pl.CostEstimate(flops=int(flops), bytes_accessed=int(moved), transcendentals=0)


def poly(coefs, z):
    out = jnp.full_like(z, coefs[-1])
    for c in coefs[-2::-1]:
        out = out * z + c
    return out


def sincos(theta):
    n = jnp.floor(theta * (1.0 / math.pi) + 0.5)
    r = (theta - n * PI_A) - n * PI_B
    z = r * r
    return r * poly(SIN, z), poly(COS, z)


def prep_kernel(feat, low, high, alpha, taps, factor, rows):
    frames = feat.shape[0]
    outs = frames // STRIDE
    a = alpha[...]
    inv = 1.0 / a

    def snake(values):
        wide = values.astype(F32)
        s, c = sincos(a * wide)
        return (wide + s * s * inv).astype(BF).astype(F32), 1.0 + 2.0 * s * c

    rows[0:8, :] = snake(low[8:16, :])[0]
    rows[frames + 8 : frames + 16, :] = snake(high[0:8, :])[0]
    step = 256

    def body(at, carry):
        here = pl.multiple_of(at * step, step)
        act, fac = snake(feat[pl.ds(here, step), :])
        rows[pl.ds(here + 8, step), :] = act
        factor[pl.ds(here, step), :] = fac
        return carry

    lax.fori_loop(0, frames // step, body, 0)
    for k in range(TAPS):
        taps[:, k * 128 : (k + 1) * 128] = rows[pl.ds(4 + k, outs, stride=STRIDE), :].astype(BF)


def prep(feat, low, high, alpha):
    frames, chans = feat.shape
    return pl.pallas_call(
        prep_kernel,
        out_shape=(
            jax.ShapeDtypeStruct((frames // STRIDE, TAPS * chans), BF),
            jax.ShapeDtypeStruct((frames, chans), F32),
        ),
        in_specs=[VMEM] * 4,
        out_specs=(VMEM, VMEM),
        scratch_shapes=[pltpu.VMEM((frames + 16, chans), F32)],
        compiler_params=params(),
        cost_estimate=cost(frames * chans * 60, frames * chans * 10),
        name="prep",
    )(feat, low, high, alpha)


def kernel_grad_kernel(which, taps, g0, g1, g2, g3, out):
    cols = g0.shape[1]
    half = cols // 2
    row = lax.broadcasted_iota(jnp.int32, (half, cols), 0)
    col = lax.broadcasted_iota(jnp.int32, (half, cols), 1)
    want = (row // 16) * 32 + which[0] * 16 + row % 16
    pick = jnp.where(col == want, 1.0, 0.0).astype(BF)
    for d, g in enumerate((g0, g1, g2, g3)):
        lhs = lax.dot_general(
            pick, g[...], (((1,), (1,)), ((), ())), preferred_element_type=F32
        ).astype(BF)
        for n in range(0, taps.shape[1], 512):
            out[d * half : (d + 1) * half, n : n + 512] = jnp.dot(
                lhs, taps[:, n : n + 512], preferred_element_type=F32
            ).astype(out.dtype)


def kernel_grad(which, taps, gs, dtype, name):
    rows = 2 * gs[0].shape[1]
    return pl.pallas_call(
        kernel_grad_kernel,
        out_shape=jax.ShapeDtypeStruct((rows, taps.shape[1]), dtype),
        in_specs=[SMEM] + [VMEM] * 5,
        out_specs=VMEM,
        compiler_params=params(),
        cost_estimate=cost(2 * rows * taps.shape[0] * taps.shape[1], 9e6),
        name=name,
    )(which, taps, *gs)


def encode_kernel(place, taps, own_w, *refs):
    pieces, (out, weights, sem) = refs[:8], refs[8:]
    copies = []

    def copy(src, row, size, d):
        c = pltpu.make_async_copy(
            src,
            weights.at[pl.ds(row, size), d * 256 : (d + 1) * 256],
            sem.at[len(copies)],
        )
        c.start()
        copies.append(c)

    copy(own_w, 0, 2048, 0)
    for n, piece in enumerate(pieces):
        row = pl.multiple_of(place[n] * 256, 256)
        for d in range(3):
            copy(piece.at[d], row, 256, d + 1)
    for c in copies:
        c.wait()
    for n in range(1024 // 256):
        for m in range(0, 768, 256):
            out[n, m : m + 256, :] = jnp.dot(
                taps[m : m + 256, :],
                weights[:, n * 256 : (n + 1) * 256],
                preferred_element_type=F32,
            ).astype(BF)


def encode(place, taps, own_w, pieces):
    return pl.pallas_call(
        encode_kernel,
        out_shape=(
            jax.ShapeDtypeStruct((4, 768, 256), BF),
            jax.ShapeDtypeStruct((2048, 1024), BF),
        ),
        in_specs=[SMEM, VMEM] + [ANY] * 9,
        out_specs=(VMEM, VMEM),
        scratch_shapes=[pltpu.SemaphoreType.DMA((25,))],
        compiler_params=params(),
        cost_estimate=cost(2 * 768 * 2048 * 1024, 13e6),
        name="encode",
    )(place, taps, own_w, *pieces)


def input_grad_kernel(g0, g1, g2, g3, edge, weights, factor, out, full, rows):
    outs = g0.shape[0]
    frames = out.shape[0]
    for d, g in enumerate((g0, g1, g2, g3)):
        full[0:outs, d * 256 : (d + 1) * 256] = g[...]
    full[outs : outs + 16, :] = edge[...]
    rows[frames : frames + 16, :] = jnp.zeros((16, 128), F32)
    for pair in range(TAPS // 2):
        res = lax.dot_general(
            full[...],
            weights[pair * 256 : (pair + 1) * 256, :],
            (((1,), (1,)), ((), ())),
            preferred_element_type=F32,
        )
        for side in range(2):
            k = 2 * pair + side
            part = res[:, side * 128 : (side + 1) * 128]
            at = pl.ds(4 + k, outs, stride=STRIDE)
            if k < STRIDE:
                rows[at, :] = part[:outs]
                if k < 4:
                    rows[frames + 4 + k : frames + 5 + k, :] = part[outs + 8 : outs + 9]
            else:
                if k < 12:
                    rows[at, :] = rows[at, :] + part[:outs]
                else:
                    rows[k - 4 : k - 3, :] = rows[k - 4 : k - 3, :] + part[outs : outs + 1]
                    rows[at, :] = rows[at, :] + part[:outs]
    step = 512
    for at in range(0, frames, step):
        out[at : at + step, :] = (
            rows[at + 8 : at + 8 + step, :] * factor[at : at + step, :]
        ).astype(BF)


def input_grad(gs, edge, weights, factor):
    frames, chans = factor.shape
    return pl.pallas_call(
        input_grad_kernel,
        out_shape=jax.ShapeDtypeStruct((frames, chans), BF),
        in_specs=[VMEM] * 7,
        out_specs=VMEM,
        scratch_shapes=[
            pltpu.VMEM((frames // STRIDE + 16, 1024), BF),
            pltpu.VMEM((frames + 16, chans), F32),
        ],
        compiler_params=params(),
        cost_estimate=cost(2 * 784 * 2048 * 1024, 13e6),
        name="input_grad",
    )(*gs, edge, weights, factor)


def turn(value, axis, by):
    count = lax.axis_size(axis)
    return lax.ppermute(value, axis, [(i, (i + by) % count) for i in range(count)])


def beside(value, by):
    count = math.prod(lax.axis_size(a) for a in TM)
    pairs = [(i, i + by) for i in range(count) if 0 <= i + by < count]
    return lax.ppermute(value, TM, pairs)


def shards(features, snake_alpha, down_weight, grad_out):
    x, z, core, y = (lax.axis_index(a) for a in ("x", "z", "core", "chan"))

    from_left = turn(grad_out, "chan", 1)
    from_right = turn(grad_out, "chan", -1)
    from_far = turn(grad_out, "chan", 2)
    gs = (grad_out, from_right, from_far, from_left)

    pair = x * 2 + core
    mine = lax.dynamic_slice(down_weight, (0, 2 * pair, 0), (512, 2, 256))
    mine = mine.reshape(4, 128, 2, 256).transpose(0, 2, 1, 3).reshape(4, 256, 256)

    def for_block(s):
        return lax.dynamic_index_in_dim(mine, (y + s) % 4, 0, keepdims=False)

    w3 = turn(for_block(1), "chan", 1)
    w1 = turn(for_block(3), "chan", -1)
    w2 = turn(for_block(2), "chan", 2)
    base = jnp.stack([w1, w2, w3])

    low = beside(features[-16:], 1)
    high = beside(features[:16], -1)
    taps, factor = prep(features, low, high, snake_alpha.reshape(1, -1))

    pieces = [base, turn(base, "x", -1), turn(base, "x", 1), turn(base, "x", 2)]
    places = [pair, ((x + 1) % 4) * 2 + core, ((x + 3) % 4) * 2 + core, ((x + 2) % 4) * 2 + core]
    pieces = pieces + [turn(p, "core", 1) for p in pieces]
    places = places + [p + 1 - 2 * core for p in places]

    own_w = lax.dynamic_slice(down_weight, (128 * y, 0, 0), (128, 16, 256))
    own_w = own_w.transpose(1, 0, 2).reshape(2048, 256)

    send = kernel_grad((1 - core).reshape(1), taps, gs, BF, "kernel_grad_send")
    got = turn(send, "core", 1)
    keep = kernel_grad(core.reshape(1), taps, gs, F32, "kernel_grad_keep")

    def for_x(e):
        at = ((x + e + 4 - y) % 4) * 128
        return lax.dynamic_slice(keep, (at, 0), (128, 2048)) + lax.dynamic_slice(
            got, (at, 0), (128, 2048)
        ).astype(F32)

    right = turn(for_x(1).astype(BF), "x", 1)
    left = turn(for_x(3).astype(BF), "x", -1)
    far = turn(for_x(2).astype(BF), "x", 2)

    partial, weights = encode(jnp.stack(places).astype(jnp.int32), taps, own_w, pieces)
    e3 = turn(partial[1], "chan", 1)
    e1 = turn(partial[3], "chan", -1)
    e2 = turn(partial[2], "chan", 2)

    last = jnp.concatenate([g[-1:] for g in gs], axis=1)
    first = jnp.concatenate([g[:1] for g in gs], axis=1)
    fill = jnp.zeros((7, 1024), BF)
    edge = jnp.concatenate([beside(last, 1), fill, beside(first, -1), fill])
    grad_features = input_grad(gs, edge, weights, factor)

    encoded = (
        partial[0].astype(F32) + e1.astype(F32) + e2.astype(F32) + e3.astype(F32)
    ).astype(BF)

    lines = (for_x(0) + right.astype(F32) + left.astype(F32) + far.astype(F32)).astype(BF)
    spread = lax.all_to_all(lines.reshape(8, 16, 2048), "z", 0, 0)
    scale = 1.0 / math.sqrt(features.shape[0] // STRIDE * 64)
    summed = jnp.sum(spread.astype(F32), axis=0) * scale
    grad_down = summed.astype(BF).reshape(16, 16, 128)
    return (encoded, grad_features, grad_down)


def solution(mesh):
    tm, chan = mesh.shape["tm"], mesh.shape["chan"]
    fine = Mesh(mesh.devices.reshape(4, tm // 8, 2, chan), (*TM, "chan"))
    placed = (P(TM, "chan"), P("chan"), P(None, None, "chan"), P(TM, "chan"))
    return jax.shard_map(
        shards,
        mesh=fine,
        in_specs=placed,
        out_specs=(P(TM, "chan"), P(TM, "chan"), P(TM, None, "chan")),
        check_vma=False,
    )
```

```python
import functools
import math

import jax
import jax.numpy as jnp
from jax import lax
from jax.experimental import pallas as pl
from jax.experimental.pallas import tpu as pltpu
from jax.sharding import Mesh
from jax.sharding import PartitionSpec as P

STRIDE = 8
TAPS = 16
BF = jnp.bfloat16
F32 = jnp.float32
TM = ("x", "z", "core")
SIN = (1.0, -1.66666666e-01, 8.33333079e-03, -1.98408371e-04, 2.75240247e-06, -2.38669497e-08)
COS = (
    1.0,
    -0.5,
    4.16666665e-02,
    -1.38888838e-03,
    2.48010074e-05,
    -2.75233926e-07,
    1.98888297e-09,
)
PI_A = 3.140625
PI_B = math.pi - PI_A
VMEM = pl.BlockSpec(memory_space=pltpu.VMEM)
SMEM = pl.BlockSpec(memory_space=pltpu.SMEM)
ANY = pl.BlockSpec(memory_space=pl.ANY)
NN = (((1,), (0,)), ((), ()))
NT = (((1,), (1,)), ((), ()))


def mul(lhs, rhs, dims=NN):
    return lax.dot_general(lhs, rhs, dims, preferred_element_type=F32)


def call(kernel, outs, specs, name, scratch=(), limit=16):
    return pl.pallas_call(
        kernel,
        out_shape=outs,
        in_specs=specs,
        out_specs=jax.tree.map(lambda _: VMEM, outs),
        scratch_shapes=scratch,
        compiler_params=pltpu.CompilerParams(vmem_limit_bytes=limit * 2**20),
        cost_estimate=pl.CostEstimate(flops=int(TIME[name] * 5.75e9), bytes_accessed=1000, transcendentals=0),
        name=name,
    )


def shape(dims, dtype=BF):
    return jax.ShapeDtypeStruct(dims, dtype)


TOKEN = shape((8, 128), F32)


TIME = dict(
    prep=7,
    weights=4,
    kernel_grad_send=3,
    kernel_grad_keep=4,
    join=1,
    encode=5,
    input_grad=6,
)


def poly(coefs, z):
    out = z * coefs[-1] + coefs[-2]
    for c in coefs[-3::-1]:
        out = out * z + c
    return out


def sincos(theta):
    n = jnp.floor(theta * (1.0 / math.pi) + 0.5)
    r = (theta - n * PI_A) - n * PI_B
    z = r * r
    return r * poly(SIN, z), poly(COS, z)


def prep_kernel(step, feat, low, high, alpha, after, taps, factor, rows):
    frames = feat.shape[0]
    a = alpha[...]
    inv = 1.0 / a

    def snake(values):
        wide = values.astype(F32)
        s, c = sincos(a * wide)
        return wide + s * s * inv, 1.0 + 2.0 * s * c

    rows[0:8, :] = snake(low[8:16, :])[0]
    rows[frames + 8 : frames + 16, :] = snake(high[0:8, :])[0]

    def body(at, carry):
        here = pl.multiple_of(at * step, step)
        act, fac = snake(feat[pl.ds(here, step), :])
        rows[pl.ds(here + 8, step), :] = act
        factor[pl.ds(here, step), :] = fac
        return carry

    lax.fori_loop(0, frames // step, body, 0)
    outs = frames // STRIDE
    for k in range(TAPS):
        taps[:, k * 128 : (k + 1) * 128] = rows[pl.ds(4 + k, outs, stride=STRIDE), :].astype(BF)


def prep(feat, low, high, alpha, after, step=256):
    frames, chans = feat.shape
    return call(
        functools.partial(prep_kernel, step),
        (shape((frames // STRIDE, TAPS * chans)), shape((frames, chans), F32)),
        [VMEM] * 5,
        "prep",
        [pltpu.VMEM((frames + 16, chans), F32)],
        limit=16,
    )(feat, low, high, alpha, after)


def weights_kernel(place, whole, own, p1, p2, p3, done, buf, rows, sem):
    y, core = place[0], place[1]
    copies = [
        pltpu.make_async_copy(
            whole.at[pl.ds(pl.multiple_of(lax.rem(y + s, 4) * 128, 128), 128)], buf.at[s], sem.at[s]
        )
        for s in range(4)
    ]
    for c in copies:
        c.start()
    for s, out in ((1, p1), (3, p3), (2, p2), (0, own)):
        copies[s].wait()
        count = TAPS if s == 0 else TAPS // 2
        for h in range(2):
            lanes = slice(h * 128, h * 128 + 128)
            rows[...] = buf[s, :, :, lanes].astype(F32).reshape(128 * TAPS, 128)
            for k in range(count):
                tap = k if s == 0 else TAPS // 2 * core + k
                out[k * 128 : (k + 1) * 128, lanes] = rows[
                    pl.ds(tap, 128, stride=TAPS), :
                ].astype(BF)
    done[...] = jnp.zeros(done.shape, F32)


def weights(place, whole):
    return call(
        weights_kernel,
        (shape((2048, 256)),) + (shape((1024, 256)),) * 3 + (TOKEN,),
        [SMEM, ANY],
        "weights",
        [
            pltpu.VMEM((4, 128, TAPS, 256), BF),
            pltpu.VMEM((128 * TAPS, 128), F32),
            pltpu.SemaphoreType.DMA((4,)),
        ],
        limit=14,
    )(place, whole)


def choose(gs, which, order, lhs):
    row = lax.broadcasted_iota(jnp.int32, (128, 256), 0)
    col = lax.broadcasted_iota(jnp.int32, (128, 256), 1)
    want = (row // 16) * 32 + which * 16 + row % 16
    pick = jnp.where(col == want, 1.0, 0.0).astype(BF)
    for d, g in enumerate(gs):
        at = pl.multiple_of(order[d] * 128, 128)
        lhs[pl.ds(at, 128), :] = mul(pick, g[...], NT).astype(BF)


def send_kernel(place, taps, g0, g1, g2, g3, out, first, last, lhs):
    choose((g0, g1, g2, g3), 1 - place[0], [place[1 + d] for d in range(4)], lhs)
    for n in range(0, 2048, 256):
        out[:, n : n + 256] = mul(lhs[...], taps[:, n : n + 256]).astype(BF)
    for d, g in enumerate((g0, g1, g2, g3)):
        first[:, d * 256 : (d + 1) * 256] = g[0:16, :]
        last[:, d * 256 : (d + 1) * 256] = g[752:768, :]


def send(place, taps, gs):
    return call(
        send_kernel,
        (shape((512, 2048)), shape((16, 1024)), shape((16, 1024))),
        [SMEM] + [VMEM] * 5,
        "kernel_grad_send",
        [pltpu.VMEM((512, 768), BF)],
        limit=12,
    )(place, taps, *gs)


def keep_kernel(place, taps, g0, g1, g2, g3, got, out, done, lhs):
    choose((g0, g1, g2, g3), place[0], [place[1 + d] for d in range(4)], lhs)
    for n in range(0, 2048, 256):
        cols = slice(n, n + 256)
        both = mul(lhs[...], taps[:, cols]) + got[:, cols].astype(F32)
        for to in range(4):
            out[to, :, cols] = both[to * 128 : (to + 1) * 128].astype(BF)
    done[...] = jnp.zeros(done.shape, F32)


def keep(place, taps, gs, got):
    return call(
        keep_kernel,
        (shape((4, 128, 2048)), TOKEN),
        [SMEM] + [VMEM] * 6,
        "kernel_grad_keep",
        [pltpu.VMEM((512, 768), BF)],
        limit=16,
    )(place, taps, *gs, got)


def join_kernel(a1, a2, a3, after, o1, o2, o3):
    for a, out in ((a1, o1), (a2, o2), (a3, o3)):
        out[...] = a[...]


def join(near, after):
    return call(join_kernel, (shape((1024, 256)),) * 3, [VMEM] * 4, "join", limit=8)(*near, after)


def encode_kernel(place, taps, own, first, last, a1, a2, a3, b1, b2, b3, out, full, o_first, o_last):
    y, core = place[0], place[1]
    here = pl.multiple_of(core * 1024, 1024)
    there = pl.multiple_of(1024 - core * 1024, 1024)
    full[:, 0:256] = own[...]
    for d, (a, b) in enumerate(((a1, b1), (a2, b2), (a3, b3))):
        cols = slice(256 * (d + 1), 256 * (d + 2))
        full[pl.ds(here, 1024), cols] = a[...]
        full[pl.ds(there, 1024), cols] = b[...]
    for d in range(4):
        out[lax.rem(y + d, 4)] = mul(taps[...], full[:, d * 256 : (d + 1) * 256]).astype(BF)
    o_first[...] = first[...]
    o_last[...] = last[...]


def encode(place, taps, own, edges, near, far):
    return call(
        encode_kernel,
        (shape((4, 768, 256)), shape((2048, 1024))) + (shape((16, 1024)),) * 2,
        [SMEM] + [VMEM] * 10,
        "encode",
        limit=20,
    )(place, taps, own, *edges, *near, *far)


def input_grad_kernel(g0, g1, g2, g3, low, high, weights, factor, after, out, full, rows):
    outs = g0.shape[0]
    frames = out.shape[0]
    for d, g in enumerate((g0, g1, g2, g3)):
        full[0:outs, d * 256 : (d + 1) * 256] = g[...]
    full[outs : outs + 16, :] = low[...]
    full[outs + 16 : outs + 32, :] = high[...]
    rows[frames : frames + 16, :] = jnp.zeros((16, 128), F32)
    for pair in range(TAPS // 2):
        res = mul(full[...], weights[pair * 256 : (pair + 1) * 256, :], NT)
        for side in range(2):
            k = 2 * pair + side
            part = res[:, side * 128 : (side + 1) * 128]
            at = pl.ds(4 + k, outs, stride=STRIDE)
            if k < STRIDE:
                rows[at, :] = part[:outs]
                if k < 4:
                    rows[frames + 4 + k : frames + 5 + k, :] = part[outs + 16 : outs + 17]
            else:
                if k >= 12:
                    rows[k - 4 : k - 3, :] = rows[k - 4 : k - 3, :] + part[outs + 15 : outs + 16]
                rows[at, :] = rows[at, :] + part[:outs]
    step = 512
    for at in range(0, frames, step):
        out[at : at + step, :] = (
            rows[at + 8 : at + 8 + step, :] * factor[at : at + step, :]
        ).astype(BF)


def input_grad(gs, low, high, weights, factor, after):
    frames, chans = factor.shape
    return call(
        input_grad_kernel,
        shape((frames, chans)),
        [VMEM] * 9,
        "input_grad",
        [pltpu.VMEM((frames // STRIDE + 32, 1024), BF), pltpu.VMEM((frames + 16, chans), F32)],
        limit=22,
    )(*gs, low, high, weights, factor, after)


def turn(value, axis, by):
    count = lax.axis_size(axis)
    return lax.ppermute(value, axis, [(i, (i + by) % count) for i in range(count)])


def beside(value, by):
    count = math.prod(lax.axis_size(a) for a in TM)
    pairs = [(i, i + by) for i in range(count) if 0 <= i + by < count]
    return lax.ppermute(value, TM, pairs)


def shards(features, snake_alpha, down_weight, grad_out):
    x, z, core, y = (lax.axis_index(a).astype(jnp.int32) for a in ("x", "z", "core", "chan"))

    gs = (
        grad_out,
        turn(grad_out, "chan", -1),
        turn(grad_out, "chan", 2),
        turn(grad_out, "chan", 1),
    )
    low, high = beside(features[-16:], 1), beside(features[:16], -1)

    at = jnp.stack([y, core])
    own, p1, p2, p3, done = weights(at, down_weight)
    near = (turn(p3, "chan", -1), turn(p2, "chan", 2), turn(p1, "chan", 1))
    taps, factor = prep(features, low, high, snake_alpha.reshape(1, -1), done)

    place = jnp.stack([core] + [(y + d) % 4 for d in range(4)])
    out, first, last = send(place, taps, gs)
    got = turn(out, "core", 1)
    kept, done = keep(place, taps, gs, got)
    summed = lax.psum_scatter(kept, "x", scatter_dimension=0)

    held = join(near, done)
    far = [turn(h, "core", 1) for h in held]
    partial, full, first, last = encode(at, taps, own, (first, last), held, far)
    edges = beside(last, 1), beside(first, -1)
    encoded = lax.psum_scatter(partial, "chan", scatter_dimension=0)
    spread = lax.all_to_all(summed.reshape(8, 16, 2048), "z", 0, 0)
    grad_features = input_grad(gs, *edges, full, factor, summed)

    scale = 1.0 / math.sqrt(features.shape[0] // STRIDE * 64)
    total = jnp.sum(spread.astype(F32), axis=0) * scale
    grad_down = total.astype(BF).reshape(16, 16, 128)
    return (encoded, grad_features, grad_down)


def solution(mesh):
    tm, chan = mesh.shape["tm"], mesh.shape["chan"]
    fine = Mesh(mesh.devices.reshape(4, tm // 8, 2, chan), (*TM, "chan"))
    placed = (P(TM, "chan"), P("chan"), P(None, None, "chan"), P(TM, "chan"))
    return jax.shard_map(
        shards,
        mesh=fine,
        in_specs=placed,
        out_specs=(P(TM, "chan"), P(TM, "chan"), P(TM, None, "chan")),
        check_vma=False,
    )
```

```python
import functools
import math

import jax
import jax.numpy as jnp
from jax import lax
from jax.experimental import pallas as pl
from jax.experimental.pallas import tpu as pltpu
from jax.sharding import Mesh
from jax.sharding import PartitionSpec as P

STRIDE = 8
TAPS = 16
BF = jnp.bfloat16
F32 = jnp.float32
TM = ("x", "z", "core")
SIN = (1.0, -1.66666666e-01, 8.33333079e-03, -1.98408371e-04, 2.75240247e-06, -2.38669497e-08)
COS = (
    1.0,
    -0.5,
    4.16666665e-02,
    -1.38888838e-03,
    2.48010074e-05,
    -2.75233926e-07,
    1.98888297e-09,
)
PI_A = 3.140625
PI_B = math.pi - PI_A
VMEM = pl.BlockSpec(memory_space=pltpu.VMEM)
SMEM = pl.BlockSpec(memory_space=pltpu.SMEM)
HBM = pl.BlockSpec(memory_space=pltpu.HBM)
NN = (((1,), (0,)), ((), ()))
NT = (((1,), (1,)), ((), ()))


def mul(lhs, rhs, dims=NN):
    return lax.dot_general(lhs, rhs, dims, preferred_element_type=F32)


def call(kernel, outs, specs, name, scratch=(), limit=16):
    return pl.pallas_call(
        kernel,
        out_shape=outs,
        in_specs=specs,
        out_specs=jax.tree.map(lambda _: VMEM, outs),
        scratch_shapes=scratch,
        compiler_params=pltpu.CompilerParams(vmem_limit_bytes=limit * 2**20),
        cost_estimate=pl.CostEstimate(flops=int(TIME[name] * FACTOR * 1.15e9), bytes_accessed=1000, transcendentals=0),
        name=name,
    )


def shape(dims, dtype=BF):
    return jax.ShapeDtypeStruct(dims, dtype)


TOKEN = shape((8, 128), F32)


FACTOR = 0.1
TIME = dict(
    prep=7,
    weights=4,
    kernel_grad_send=3,
    kernel_grad_keep=4,
    join=1,
    encode=5,
    lines=1,
    input_grad=6,
)


def poly(coefs, z):
    out = z * coefs[-1] + coefs[-2]
    for c in coefs[-3::-1]:
        out = out * z + c
    return out


def sincos(theta):
    n = jnp.floor(theta * (1.0 / math.pi) + 0.5)
    r = (theta - n * PI_A) - n * PI_B
    z = r * r
    return r * poly(SIN, z), poly(COS, z)


def prep_kernel(step, feat, low, high, alpha, after, taps, factor, rows):
    frames = feat.shape[0]
    a = alpha[...]
    inv = 1.0 / a

    def snake(values):
        wide = values.astype(F32)
        s, c = sincos(a * wide)
        return wide + s * s * inv, 1.0 + 2.0 * s * c

    rows[0:8, :] = snake(low[8:16, :])[0]
    rows[frames + 8 : frames + 16, :] = snake(high[0:8, :])[0]

    def body(at, carry):
        here = pl.multiple_of(at * step, step)
        act, fac = snake(feat[pl.ds(here, step), :])
        rows[pl.ds(here + 8, step), :] = act
        factor[pl.ds(here, step), :] = fac
        return carry

    lax.fori_loop(0, frames // step, body, 0)
    outs = frames // STRIDE
    for k in range(TAPS):
        taps[:, k * 128 : (k + 1) * 128] = rows[pl.ds(4 + k, outs, stride=STRIDE), :].astype(BF)


def prep(feat, low, high, alpha, after, step=256):
    frames, chans = feat.shape
    return call(
        functools.partial(prep_kernel, step),
        (shape((frames // STRIDE, TAPS * chans)), shape((frames, chans), F32)),
        [VMEM] * 5,
        "prep",
        [pltpu.VMEM((frames + 16, chans), F32)],
        limit=16,
    )(feat, low, high, alpha, after)


def weights_kernel(place, whole, own, p1, p2, p3, done, buf, rows, sem):
    y, core = place[0], place[1]
    copies = [
        pltpu.make_async_copy(
            whole.at[pl.ds(pl.multiple_of(lax.rem(y + s, 4) * 128, 128), 128)], buf.at[s], sem.at[s]
        )
        for s in range(4)
    ]
    for c in copies:
        c.start()
    for s, out in ((1, p1), (3, p3), (2, p2), (0, own)):
        copies[s].wait()
        count = TAPS if s == 0 else TAPS // 2
        for h in range(2):
            lanes = slice(h * 128, h * 128 + 128)
            rows[...] = buf[s, :, :, lanes].astype(F32).reshape(128 * TAPS, 128)
            for k in range(count):
                tap = k if s == 0 else TAPS // 2 * core + k
                out[k * 128 : (k + 1) * 128, lanes] = rows[
                    pl.ds(tap, 128, stride=TAPS), :
                ].astype(BF)
    done[...] = jnp.zeros(done.shape, F32)


def weights(place, whole):
    return call(
        weights_kernel,
        (shape((2048, 256)),) + (shape((1024, 256)),) * 3 + (TOKEN,),
        [SMEM, HBM],
        "weights",
        [
            pltpu.VMEM((4, 128, TAPS, 256), BF),
            pltpu.VMEM((128 * TAPS, 128), F32),
            pltpu.SemaphoreType.DMA((4,)),
        ],
        limit=14,
    )(place, whole)


def choose(gs, which, order, lhs):
    row = lax.broadcasted_iota(jnp.int32, (128, 256), 0)
    col = lax.broadcasted_iota(jnp.int32, (128, 256), 1)
    want = (row // 16) * 32 + which * 16 + row % 16
    pick = jnp.where(col == want, 1.0, 0.0).astype(BF)
    for d, g in enumerate(gs):
        at = pl.multiple_of(order[d] * 128, 128)
        lhs[pl.ds(at, 128), :] = mul(pick, g[...], NT).astype(BF)


def send_kernel(place, taps, g0, g1, g2, g3, out, first, last, lhs):
    choose((g0, g1, g2, g3), 1 - place[0], [place[1 + d] for d in range(4)], lhs)
    for n in range(0, 2048, 256):
        out[:, n : n + 256] = mul(lhs[...], taps[:, n : n + 256]).astype(BF)
    for d, g in enumerate((g0, g1, g2, g3)):
        first[:, d * 256 : (d + 1) * 256] = g[0:16, :]
        last[:, d * 256 : (d + 1) * 256] = g[752:768, :]


def send(place, taps, gs):
    return call(
        send_kernel,
        (shape((512, 2048)), shape((16, 1024)), shape((16, 1024))),
        [SMEM] + [VMEM] * 5,
        "kernel_grad_send",
        [pltpu.VMEM((512, 768), BF)],
        limit=12,
    )(place, taps, *gs)


def keep_kernel(place, taps, g0, g1, g2, g3, got, o0, o1, o2, o3, done, lhs):
    choose((g0, g1, g2, g3), place[0], [place[1 + d] for d in range(4)], lhs)
    for n in range(0, 2048, 256):
        cols = slice(n, n + 256)
        both = mul(lhs[...], taps[:, cols]) + got[:, cols].astype(F32)
        o0[:, cols] = both[0:128]
        o1[:, cols] = both[128:256].astype(BF)
        o2[:, cols] = both[256:384].astype(BF)
        o3[:, cols] = both[384:512].astype(BF)
    done[...] = jnp.zeros(done.shape, F32)


def keep(place, taps, gs, got):
    return call(
        keep_kernel,
        (shape((128, 2048), F32),) + (shape((128, 2048)),) * 3 + (TOKEN,),
        [SMEM] + [VMEM] * 6,
        "kernel_grad_keep",
        [pltpu.VMEM((512, 768), BF)],
        limit=16,
    )(place, taps, *gs, got)


def join_kernel(a1, a2, a3, after, o1, o2, o3):
    for a, out in ((a1, o1), (a2, o2), (a3, o3)):
        out[...] = a[...]


def join(near, after):
    return call(join_kernel, (shape((1024, 256)),) * 3, [VMEM] * 4, "join", limit=8)(*near, after)


def encode_kernel(
    core, taps, own, first, last, a1, a2, a3, b1, b2, b3, o0, o1, o2, o3, full, o_first, o_last
):
    here = pl.multiple_of(core[0] * 1024, 1024)
    there = pl.multiple_of(1024 - core[0] * 1024, 1024)
    full[:, 0:256] = own[...]
    for d, (a, b) in enumerate(((a1, b1), (a2, b2), (a3, b3))):
        cols = slice(256 * (d + 1), 256 * (d + 2))
        full[pl.ds(here, 1024), cols] = a[...]
        full[pl.ds(there, 1024), cols] = b[...]
    for d, out in enumerate((o0, o1, o2, o3)):
        out[...] = mul(taps[...], full[:, d * 256 : (d + 1) * 256]).astype(out.dtype)
    o_first[...] = first[...]
    o_last[...] = last[...]


def encode(core, taps, own, edges, near, far):
    return call(
        encode_kernel,
        (shape((768, 256), F32),)
        + (shape((768, 256)),) * 3
        + (shape((2048, 1024)),)
        + (shape((16, 1024)),) * 2,
        [SMEM] + [VMEM] * 10,
        "encode",
        limit=20,
    )(core, taps, own, *edges, *near, *far)


def lines_kernel(own, a1, a2, a3, out, done):
    for m in range(8):
        here = slice(m * 16, m * 16 + 16)
        out[m] = (
            own[here, :] + a1[here, :].astype(F32) + a2[here, :].astype(F32) + a3[here, :].astype(F32)
        ).astype(BF)
    done[...] = jnp.zeros(done.shape, F32)


def lines(own, arrived):
    return call(lines_kernel, (shape((8, 16, 2048)), TOKEN), [VMEM] * 4, "lines", limit=8)(
        own, *arrived
    )


def input_grad_kernel(g0, g1, g2, g3, low, high, weights, factor, after, out, full, rows):
    outs = g0.shape[0]
    frames = out.shape[0]
    for d, g in enumerate((g0, g1, g2, g3)):
        full[0:outs, d * 256 : (d + 1) * 256] = g[...]
    full[outs : outs + 16, :] = low[...]
    full[outs + 16 : outs + 32, :] = high[...]
    rows[frames : frames + 16, :] = jnp.zeros((16, 128), F32)
    for pair in range(TAPS // 2):
        res = mul(full[...], weights[pair * 256 : (pair + 1) * 256, :], NT)
        for side in range(2):
            k = 2 * pair + side
            part = res[:, side * 128 : (side + 1) * 128]
            at = pl.ds(4 + k, outs, stride=STRIDE)
            if k < STRIDE:
                rows[at, :] = part[:outs]
                if k < 4:
                    rows[frames + 4 + k : frames + 5 + k, :] = part[outs + 16 : outs + 17]
            else:
                if k >= 12:
                    rows[k - 4 : k - 3, :] = rows[k - 4 : k - 3, :] + part[outs + 15 : outs + 16]
                rows[at, :] = rows[at, :] + part[:outs]
    step = 512
    for at in range(0, frames, step):
        out[at : at + step, :] = (
            rows[at + 8 : at + 8 + step, :] * factor[at : at + step, :]
        ).astype(BF)


def input_grad(gs, low, high, weights, factor, after):
    frames, chans = factor.shape
    return call(
        input_grad_kernel,
        shape((frames, chans)),
        [VMEM] * 9,
        "input_grad",
        [pltpu.VMEM((frames // STRIDE + 32, 1024), BF), pltpu.VMEM((frames + 16, chans), F32)],
        limit=22,
    )(*gs, low, high, weights, factor, after)


def turn(value, axis, by):
    count = lax.axis_size(axis)
    return lax.ppermute(value, axis, [(i, (i + by) % count) for i in range(count)])


def beside(value, by):
    count = math.prod(lax.axis_size(a) for a in TM)
    pairs = [(i, i + by) for i in range(count) if 0 <= i + by < count]
    return lax.ppermute(value, TM, pairs)


def shards(features, snake_alpha, down_weight, grad_out):
    x, z, core, y = (lax.axis_index(a).astype(jnp.int32) for a in ("x", "z", "core", "chan"))

    gs = (
        grad_out,
        turn(grad_out, "chan", -1),
        turn(grad_out, "chan", 2),
        turn(grad_out, "chan", 1),
    )
    low, high = beside(features[-16:], 1), beside(features[:16], -1)

    at = jnp.stack([y, core])
    own, p1, p2, p3, done = weights(at, down_weight)
    near = (turn(p3, "chan", -1), turn(p2, "chan", 2), turn(p1, "chan", 1))
    taps, factor = prep(features, low, high, snake_alpha.reshape(1, -1), done)

    place = jnp.stack([core] + [(y + d + 4 - x) % 4 for d in range(4)])
    out, first, last = send(place, taps, gs)
    got = turn(out, "core", 1)
    keep0, keep1, keep2, keep3, done = keep(place, taps, gs, got)
    arrived = (turn(keep1, "x", 1), turn(keep3, "x", -1), turn(keep2, "x", 2))

    held = join(near, done)
    far = [turn(h, "core", 1) for h in held]
    mine, part1, part2, part3, full, first, last = encode(
        core.reshape(1), taps, own, (first, last), held, far
    )
    others = (turn(part1, "chan", 1), turn(part3, "chan", -1), turn(part2, "chan", 2))
    edges = beside(last, 1), beside(first, -1)
    summed, done = lines(keep0, arrived)
    spread = lax.all_to_all(summed, "z", 0, 0)
    grad_features = input_grad(gs, *edges, full, factor, done)

    encoded = (mine + sum(o.astype(F32) for o in others)).astype(BF)

    scale = 1.0 / math.sqrt(features.shape[0] // STRIDE * 64)
    total = jnp.sum(spread.astype(F32), axis=0) * scale
    grad_down = total.astype(BF).reshape(16, 16, 128)
    return (encoded, grad_features, grad_down)


def solution(mesh):
    tm, chan = mesh.shape["tm"], mesh.shape["chan"]
    fine = Mesh(mesh.devices.reshape(4, tm // 8, 2, chan), (*TM, "chan"))
    placed = (P(TM, "chan"), P("chan"), P(None, None, "chan"), P(TM, "chan"))
    return jax.shard_map(
        shards,
        mesh=fine,
        in_specs=placed,
        out_specs=(P(TM, "chan"), P(TM, "chan"), P(TM, None, "chan")),
        check_vma=False,
    )
```

```python
import functools
import math

import jax
import jax.numpy as jnp
from jax import lax
from jax.experimental import pallas as pl
from jax.experimental.pallas import tpu as pltpu
from jax.sharding import Mesh
from jax.sharding import PartitionSpec as P

STRIDE = 8
TAPS = 16
BF = jnp.bfloat16
F32 = jnp.float32
TM = ("x", "z", "core")
SIN = (1.0, -1.66666666e-01, 8.33333079e-03, -1.98408371e-04, 2.75240247e-06, -2.38669497e-08)
COS = (
    1.0,
    -0.5,
    4.16666665e-02,
    -1.38888838e-03,
    2.48010074e-05,
    -2.75233926e-07,
    1.98888297e-09,
)
PI_A = 3.140625
PI_B = math.pi - PI_A
VMEM = pl.BlockSpec(memory_space=pltpu.VMEM)
SMEM = pl.BlockSpec(memory_space=pltpu.SMEM)
HBM = pl.BlockSpec(memory_space=pltpu.HBM)
NN = (((1,), (0,)), ((), ()))
NT = (((1,), (1,)), ((), ()))


def mul(lhs, rhs, dims=NN):
    return lax.dot_general(lhs, rhs, dims, preferred_element_type=F32)


def call(kernel, outs, specs, name, scratch=(), limit=24):
    return pl.pallas_call(
        kernel,
        out_shape=outs,
        in_specs=specs,
        out_specs=jax.tree.map(lambda _: VMEM, outs),
        scratch_shapes=scratch,
        compiler_params=pltpu.CompilerParams(vmem_limit_bytes=limit * 2**20),
        cost_estimate=pl.CostEstimate(flops=int(TIME[name] * FACTOR * 1.15e9), bytes_accessed=1000, transcendentals=0),
        name=name,
    )


def shape(dims, dtype=BF):
    return jax.ShapeDtypeStruct(dims, dtype)


TOKEN = shape((8, 128), F32)


FACTOR = 0.1
TIME = dict(
    prep=7,
    weights=4,
    kernel_grad_send=3,
    kernel_grad_keep=4,
    join=1,
    encode=5,
    lines=1,
    input_grad=6,
)


def poly(coefs, z):
    out = z * coefs[-1] + coefs[-2]
    for c in coefs[-3::-1]:
        out = out * z + c
    return out


def sincos(theta):
    n = jnp.floor(theta * (1.0 / math.pi) + 0.5)
    r = (theta - n * PI_A) - n * PI_B
    z = r * r
    return r * poly(SIN, z), poly(COS, z)


def prep_kernel(step, feat, low, high, alpha, after, taps, factor, rows):
    frames = feat.shape[0]
    a = alpha[...]
    inv = 1.0 / a

    def snake(values):
        wide = values.astype(F32)
        s, c = sincos(a * wide)
        return wide + s * s * inv, 1.0 + 2.0 * s * c

    rows[0:8, :] = snake(low[8:16, :])[0]
    rows[frames + 8 : frames + 16, :] = snake(high[0:8, :])[0]

    def body(at, carry):
        here = pl.multiple_of(at * step, step)
        act, fac = snake(feat[pl.ds(here, step), :])
        rows[pl.ds(here + 8, step), :] = act
        factor[pl.ds(here, step), :] = fac
        return carry

    lax.fori_loop(0, frames // step, body, 0)
    outs = frames // STRIDE
    for k in range(TAPS):
        taps[:, k * 128 : (k + 1) * 128] = rows[pl.ds(4 + k, outs, stride=STRIDE), :].astype(BF)


def prep(feat, low, high, alpha, after, step=256):
    frames, chans = feat.shape
    return call(
        functools.partial(prep_kernel, step),
        (shape((frames // STRIDE, TAPS * chans)), shape((frames, chans), F32)),
        [VMEM] * 5,
        "prep",
        [pltpu.VMEM((frames + 16, chans), F32)],
        limit=24,
    )(feat, low, high, alpha, after)


def weights_kernel(place, whole, own, parts, done, buf, rows, sem):
    y, core = place[0], place[1]
    copies = [
        pltpu.make_async_copy(
            whole.at[pl.ds(pl.multiple_of(lax.rem(y + s, 4) * 128, 128), 128)], buf.at[s], sem.at[s]
        )
        for s in range(4)
    ]
    for c in copies:
        c.start()
    half = TAPS // 2
    for s in (1, 3, 2, 0):
        copies[s].wait()
        to = lax.rem(y + s, 4)
        for h in range(2):
            lanes = slice(h * 128, h * 128 + 128)
            rows[...] = buf[s, :, :, lanes].astype(F32).reshape(128 * TAPS, 128)
            for k in range(half):
                parts[to, k * 128 : (k + 1) * 128, lanes] = rows[
                    pl.ds(half * core + k, 128, stride=TAPS), :
                ].astype(BF)
            if s == 0:
                for k in range(TAPS):
                    own[k * 128 : (k + 1) * 128, lanes] = rows[
                        pl.ds(k, 128, stride=TAPS), :
                    ].astype(BF)
    done[...] = jnp.zeros(done.shape, F32)


def weights(place, whole):
    return call(
        weights_kernel,
        (shape((2048, 256)), shape((4, 1024, 256)), TOKEN),
        [SMEM, HBM],
        "weights",
        [
            pltpu.VMEM((4, 128, TAPS, 256), BF),
            pltpu.VMEM((128 * TAPS, 128), F32),
            pltpu.SemaphoreType.DMA((4,)),
        ],
        limit=24,
    )(place, whole)


def choose(gs, which, order, lhs):
    row = lax.broadcasted_iota(jnp.int32, (128, 256), 0)
    col = lax.broadcasted_iota(jnp.int32, (128, 256), 1)
    want = (row // 16) * 32 + which * 16 + row % 16
    pick = jnp.where(col == want, 1.0, 0.0).astype(BF)
    for d, g in enumerate(gs):
        at = pl.multiple_of(order[d] * 128, 128)
        lhs[pl.ds(at, 128), :] = mul(pick, g[...], NT).astype(BF)


def send_kernel(place, taps, g0, g1, g2, g3, out, first, last, lhs):
    choose((g0, g1, g2, g3), 1 - place[0], [place[1 + d] for d in range(4)], lhs)
    for n in range(0, 2048, 256):
        out[:, n : n + 256] = mul(lhs[...], taps[:, n : n + 256]).astype(BF)
    for d, g in enumerate((g0, g1, g2, g3)):
        first[:, d * 256 : (d + 1) * 256] = g[0:16, :]
        last[:, d * 256 : (d + 1) * 256] = g[752:768, :]


def send(place, taps, gs):
    return call(
        send_kernel,
        (shape((512, 2048)), shape((16, 1024)), shape((16, 1024))),
        [SMEM] + [VMEM] * 5,
        "kernel_grad_send",
        [pltpu.VMEM((512, 768), BF)],
        limit=24,
    )(place, taps, *gs)


def keep_kernel(place, taps, g0, g1, g2, g3, got, o0, o1, o2, o3, done, lhs):
    choose((g0, g1, g2, g3), place[0], [place[1 + d] for d in range(4)], lhs)
    for n in range(0, 2048, 256):
        cols = slice(n, n + 256)
        both = mul(lhs[...], taps[:, cols]) + got[:, cols].astype(F32)
        o0[:, cols] = both[0:128]
        o1[:, cols] = both[128:256].astype(BF)
        o2[:, cols] = both[256:384].astype(BF)
        o3[:, cols] = both[384:512].astype(BF)
    done[...] = jnp.zeros(done.shape, F32)


def keep(place, taps, gs, got):
    return call(
        keep_kernel,
        (shape((128, 2048), F32),) + (shape((128, 2048)),) * 3 + (TOKEN,),
        [SMEM] + [VMEM] * 6,
        "kernel_grad_keep",
        [pltpu.VMEM((512, 768), BF)],
        limit=24,
    )(place, taps, *gs, got)


def join_kernel(y, parts, after, o1, o2, o3):
    for d, out in ((1, o1), (2, o2), (3, o3)):
        out[...] = parts[lax.rem(y[0] + d, 4)]


def join(y, parts, after):
    return call(join_kernel, (shape((1024, 256)),) * 3, [SMEM, VMEM, VMEM], "join", limit=24)(
        y, parts, after
    )


def encode_kernel(
    core, taps, own, first, last, a1, a2, a3, b1, b2, b3, o0, o1, o2, o3, full, o_first, o_last
):
    here = pl.multiple_of(core[0] * 1024, 1024)
    there = pl.multiple_of(1024 - core[0] * 1024, 1024)
    full[:, 0:256] = own[...]
    for d, (a, b) in enumerate(((a1, b1), (a2, b2), (a3, b3))):
        cols = slice(256 * (d + 1), 256 * (d + 2))
        full[pl.ds(here, 1024), cols] = a[...]
        full[pl.ds(there, 1024), cols] = b[...]
    for d, out in enumerate((o0, o1, o2, o3)):
        out[...] = mul(taps[...], full[:, d * 256 : (d + 1) * 256]).astype(out.dtype)
    o_first[...] = first[...]
    o_last[...] = last[...]


def encode(core, taps, own, edges, near, far):
    return call(
        encode_kernel,
        (shape((768, 256), F32),)
        + (shape((768, 256)),) * 3
        + (shape((2048, 1024)),)
        + (shape((16, 1024)),) * 2,
        [SMEM] + [VMEM] * 10,
        "encode",
        limit=24,
    )(core, taps, own, *edges, *near, *far)


def lines_kernel(own, a1, a2, a3, out, done):
    for m in range(8):
        here = slice(m * 16, m * 16 + 16)
        out[m] = (
            own[here, :] + a1[here, :].astype(F32) + a2[here, :].astype(F32) + a3[here, :].astype(F32)
        ).astype(BF)
    done[...] = jnp.zeros(done.shape, F32)


def lines(own, arrived):
    return call(lines_kernel, (shape((8, 16, 2048)), TOKEN), [VMEM] * 4, "lines", limit=24)(
        own, *arrived
    )


def input_grad_kernel(g0, g1, g2, g3, low, high, weights, factor, after, out, full, rows):
    outs = g0.shape[0]
    frames = out.shape[0]
    for d, g in enumerate((g0, g1, g2, g3)):
        full[0:outs, d * 256 : (d + 1) * 256] = g[...]
    full[outs : outs + 16, :] = low[...]
    full[outs + 16 : outs + 32, :] = high[...]
    rows[frames : frames + 16, :] = jnp.zeros((16, 128), F32)
    for pair in range(TAPS // 2):
        res = mul(full[...], weights[pair * 256 : (pair + 1) * 256, :], NT)
        for side in range(2):
            k = 2 * pair + side
            part = res[:, side * 128 : (side + 1) * 128]
            at = pl.ds(4 + k, outs, stride=STRIDE)
            if k < STRIDE:
                rows[at, :] = part[:outs]
                if k < 4:
                    rows[frames + 4 + k : frames + 5 + k, :] = part[outs + 16 : outs + 17]
            else:
                if k >= 12:
                    rows[k - 4 : k - 3, :] = rows[k - 4 : k - 3, :] + part[outs + 15 : outs + 16]
                rows[at, :] = rows[at, :] + part[:outs]
    step = 512
    for at in range(0, frames, step):
        out[at : at + step, :] = (
            rows[at + 8 : at + 8 + step, :] * factor[at : at + step, :]
        ).astype(BF)


def input_grad(gs, low, high, weights, factor, after):
    frames, chans = factor.shape
    return call(
        input_grad_kernel,
        shape((frames, chans)),
        [VMEM] * 9,
        "input_grad",
        [pltpu.VMEM((frames // STRIDE + 32, 1024), BF), pltpu.VMEM((frames + 16, chans), F32)],
        limit=24,
    )(*gs, low, high, weights, factor, after)


def turn(value, axis, by):
    count = lax.axis_size(axis)
    return lax.ppermute(value, axis, [(i, (i + by) % count) for i in range(count)])


def beside(value, by):
    count = math.prod(lax.axis_size(a) for a in TM)
    pairs = [(i, i + by) for i in range(count) if 0 <= i + by < count]
    return lax.ppermute(value, TM, pairs)


def shards(features, snake_alpha, down_weight, grad_out):
    x, z, core, y = (lax.axis_index(a).astype(jnp.int32) for a in ("x", "z", "core", "chan"))

    gs = (
        grad_out,
        turn(grad_out, "chan", -1),
        turn(grad_out, "chan", 2),
        turn(grad_out, "chan", 1),
    )
    low, high = beside(features[-16:], 1), beside(features[:16], -1)

    at = jnp.stack([y, core])
    own, parts, done = weights(at, down_weight)
    near = lax.all_to_all(parts, "chan", 0, 0)
    taps, factor = prep(features, low, high, snake_alpha.reshape(1, -1), done)

    place = jnp.stack([core] + [(y + d + 4 - x) % 4 for d in range(4)])
    out, first, last = send(place, taps, gs)
    got = turn(out, "core", 1)
    keep0, keep1, keep2, keep3, done = keep(place, taps, gs, got)
    arrived = (turn(keep1, "x", 1), turn(keep3, "x", -1), turn(keep2, "x", 2))

    held = join(y.reshape(1), near, done)
    far = [turn(h, "core", 1) for h in held]
    mine, part1, part2, part3, full, first, last = encode(
        core.reshape(1), taps, own, (first, last), held, far
    )
    others = (turn(part1, "chan", 1), turn(part3, "chan", -1), turn(part2, "chan", 2))
    edges = beside(last, 1), beside(first, -1)
    summed, done = lines(keep0, arrived)
    spread = lax.all_to_all(summed, "z", 0, 0)
    grad_features = input_grad(gs, *edges, full, factor, done)

    encoded = (mine + sum(o.astype(F32) for o in others)).astype(BF)

    scale = 1.0 / math.sqrt(features.shape[0] // STRIDE * 64)
    total = jnp.sum(spread.astype(F32), axis=0) * scale
    grad_down = total.astype(BF).reshape(16, 16, 128)
    return (encoded, grad_features, grad_down)


def solution(mesh):
    tm, chan = mesh.shape["tm"], mesh.shape["chan"]
    fine = Mesh(mesh.devices.reshape(4, tm // 8, 2, chan), (*TM, "chan"))
    placed = (P(TM, "chan"), P("chan"), P(None, None, "chan"), P(TM, "chan"))
    return jax.shard_map(
        shards,
        mesh=fine,
        in_specs=placed,
        out_specs=(P(TM, "chan"), P(TM, "chan"), P(TM, None, "chan")),
        check_vma=False,
    )
```

```python
import functools
import math

import jax
import jax.numpy as jnp
from jax import lax
from jax.experimental import pallas as pl
from jax.experimental.pallas import tpu as pltpu
from jax.sharding import Mesh
from jax.sharding import PartitionSpec as P

STRIDE = 8
TAPS = 16
BF = jnp.bfloat16
F32 = jnp.float32
TM = ("x", "z", "core")
SIN = (1.0, -1.66666666e-01, 8.33333079e-03, -1.98408371e-04, 2.75240247e-06, -2.38669497e-08)
COS = (
    1.0,
    -0.5,
    4.16666665e-02,
    -1.38888838e-03,
    2.48010074e-05,
    -2.75233926e-07,
    1.98888297e-09,
)
PI_A = 3.140625
PI_B = math.pi - PI_A
VMEM = pl.BlockSpec(memory_space=pltpu.VMEM)
SMEM = pl.BlockSpec(memory_space=pltpu.SMEM)
HBM = pl.BlockSpec(memory_space=pltpu.HBM)
NN = (((1,), (0,)), ((), ()))
NT = (((1,), (1,)), ((), ()))


def mul(lhs, rhs, dims=NN):
    return lax.dot_general(lhs, rhs, dims, preferred_element_type=F32)


def call(kernel, outs, specs, name, scratch=(), limit=24):
    return pl.pallas_call(
        kernel,
        out_shape=outs,
        in_specs=specs,
        out_specs=jax.tree.map(lambda _: VMEM, outs),
        scratch_shapes=scratch,
        compiler_params=pltpu.CompilerParams(vmem_limit_bytes=limit * 2**20),
        cost_estimate=pl.CostEstimate(flops=int(TIME[name] * FACTOR * 1.15e9), bytes_accessed=1000, transcendentals=0),
        name=name,
    )


def shape(dims, dtype=BF):
    return jax.ShapeDtypeStruct(dims, dtype)


TOKEN = shape((8, 128), F32)


FACTOR = 1.3
TIME = dict(
    prep=7,
    weights=4,
    kernel_grad_send=3,
    kernel_grad_keep=4,
    join=1,
    total=1,
    encode=5,
    lines=1,
    input_grad=6,
)


def poly(coefs, z):
    out = z * coefs[-1] + coefs[-2]
    for c in coefs[-3::-1]:
        out = out * z + c
    return out


def sincos(theta):
    n = jnp.floor(theta * (1.0 / math.pi) + 0.5)
    r = (theta - n * PI_A) - n * PI_B
    z = r * r
    return r * poly(SIN, z), poly(COS, z)


def prep_kernel(step, feat, low, high, alpha, after, taps, factor, rows):
    frames = feat.shape[0]
    a = alpha[...]
    inv = 1.0 / a

    def snake(values):
        wide = values.astype(F32)
        s, c = sincos(a * wide)
        return wide + s * s * inv, 1.0 + 2.0 * s * c

    rows[0:8, :] = snake(low[8:16, :])[0]
    rows[frames + 8 : frames + 16, :] = snake(high[0:8, :])[0]

    def body(at, carry):
        here = pl.multiple_of(at * step, step)
        act, fac = snake(feat[pl.ds(here, step), :])
        rows[pl.ds(here + 8, step), :] = act
        factor[pl.ds(here, step), :] = fac
        return carry

    lax.fori_loop(0, frames // step, body, 0)
    outs = frames // STRIDE
    for k in range(TAPS):
        taps[:, k * 128 : (k + 1) * 128] = rows[pl.ds(4 + k, outs, stride=STRIDE), :].astype(BF)


def prep(feat, low, high, alpha, after, step=256):
    frames, chans = feat.shape
    return call(
        functools.partial(prep_kernel, step),
        (shape((frames // STRIDE, TAPS * chans)), shape((frames, chans), F32)),
        [VMEM] * 5,
        "prep",
        [pltpu.VMEM((frames + 16, chans), F32)],
        limit=24,
    )(feat, low, high, alpha, after)


def weights_kernel(place, whole, own, p1, p2, p3, done, buf, rows, sem):
    y, core = place[0], place[1]
    copies = [
        pltpu.make_async_copy(
            whole.at[pl.ds(pl.multiple_of(lax.rem(y + s, 4) * 128, 128), 128)], buf.at[s], sem.at[s]
        )
        for s in range(4)
    ]
    for c in copies:
        c.start()
    for s, out in ((1, p1), (3, p3), (2, p2), (0, own)):
        copies[s].wait()
        count = TAPS if s == 0 else TAPS // 2
        for h in range(2):
            lanes = slice(h * 128, h * 128 + 128)
            rows[...] = buf[s, :, :, lanes].astype(F32).reshape(128 * TAPS, 128)
            for k in range(count):
                tap = k if s == 0 else TAPS // 2 * core + k
                out[k * 128 : (k + 1) * 128, lanes] = rows[
                    pl.ds(tap, 128, stride=TAPS), :
                ].astype(BF)
    done[...] = jnp.zeros(done.shape, F32)


def weights(place, whole):
    return call(
        weights_kernel,
        (shape((2048, 256)),) + (shape((1024, 256)),) * 3 + (TOKEN,),
        [SMEM, HBM],
        "weights",
        [
            pltpu.VMEM((4, 128, TAPS, 256), BF),
            pltpu.VMEM((128 * TAPS, 128), F32),
            pltpu.SemaphoreType.DMA((4,)),
        ],
        limit=24,
    )(place, whole)


def choose(gs, which, order, lhs):
    row = lax.broadcasted_iota(jnp.int32, (128, 256), 0)
    col = lax.broadcasted_iota(jnp.int32, (128, 256), 1)
    want = (row // 16) * 32 + which * 16 + row % 16
    pick = jnp.where(col == want, 1.0, 0.0).astype(BF)
    for d, g in enumerate(gs):
        at = pl.multiple_of(order[d] * 128, 128)
        lhs[pl.ds(at, 128), :] = mul(pick, g[...], NT).astype(BF)


def send_kernel(place, taps, g0, g1, g2, g3, out, lhs):
    choose((g0, g1, g2, g3), 1 - place[0], [place[1 + d] for d in range(4)], lhs)
    for n in range(0, 2048, 256):
        out[:, n : n + 256] = mul(lhs[...], taps[:, n : n + 256]).astype(BF)


def send(place, taps, gs):
    return call(
        send_kernel,
        shape((512, 2048)),
        [SMEM] + [VMEM] * 5,
        "kernel_grad_send",
        [pltpu.VMEM((512, 768), BF)],
        limit=24,
    )(place, taps, *gs)


def keep_kernel(place, taps, g0, g1, g2, g3, got, out, done, lhs):
    choose((g0, g1, g2, g3), place[0], [place[1 + d] for d in range(4)], lhs)
    for n in range(0, 2048, 256):
        cols = slice(n, n + 256)
        both = mul(lhs[...], taps[:, cols]) + got[:, cols].astype(F32)
        for to in range(4):
            out[to, :, cols] = both[to * 128 : (to + 1) * 128].astype(BF)
    done[...] = jnp.zeros(done.shape, F32)


def keep(place, taps, gs, got):
    return call(
        keep_kernel,
        (shape((4, 128, 2048)), TOKEN),
        [SMEM] + [VMEM] * 6,
        "kernel_grad_keep",
        [pltpu.VMEM((512, 768), BF)],
        limit=24,
    )(place, taps, *gs, got)


def join_kernel(a1, a2, a3, after, o1, o2, o3):
    for a, out in ((a1, o1), (a2, o2), (a3, o3)):
        out[...] = a[...]


def join(near, after):
    return call(join_kernel, (shape((1024, 256)),) * 3, [VMEM] * 4, "join", limit=24)(*near, after)


def encode_kernel(
    core, taps, own, g0, g1, g2, g3, a1, a2, a3, b1, b2, b3, o0, o1, o2, o3, full, o_first, o_last, done
):
    here = pl.multiple_of(core[0] * 1024, 1024)
    there = pl.multiple_of(1024 - core[0] * 1024, 1024)
    full[:, 0:256] = own[...]
    for d, (a, b) in enumerate(((a1, b1), (a2, b2), (a3, b3))):
        cols = slice(256 * (d + 1), 256 * (d + 2))
        full[pl.ds(here, 1024), cols] = a[...]
        full[pl.ds(there, 1024), cols] = b[...]
    for d, out in enumerate((o0, o1, o2, o3)):
        out[...] = mul(taps[...], full[:, d * 256 : (d + 1) * 256]).astype(out.dtype)
    for d, g in enumerate((g0, g1, g2, g3)):
        o_first[:, d * 256 : (d + 1) * 256] = g[0:16, :]
        o_last[:, d * 256 : (d + 1) * 256] = g[752:768, :]
    done[...] = jnp.zeros(done.shape, F32)


def encode(core, taps, own, gs, near, far):
    return call(
        encode_kernel,
        (shape((768, 256), F32),)
        + (shape((768, 256)),) * 3
        + (shape((2048, 1024)),)
        + (shape((16, 1024)),) * 2
        + (TOKEN,),
        [SMEM] + [VMEM] * 12,
        "encode",
        limit=24,
    )(core, taps, own, *gs, *near, *far)


def lines_kernel(parts, after, out, done):
    for m in range(8):
        here = slice(m * 16, m * 16 + 16)
        out[m] = sum(parts[n, here, :].astype(F32) for n in range(4)).astype(BF)
    done[...] = jnp.zeros(done.shape, F32)


def lines(parts, after):
    return call(lines_kernel, (shape((8, 16, 2048)), TOKEN), [VMEM] * 2, "lines", limit=24)(
        parts, after
    )


def input_grad_kernel(g0, g1, g2, g3, low, high, weights, factor, after, out, done, full, rows):
    outs = g0.shape[0]
    frames = out.shape[0]
    for d, g in enumerate((g0, g1, g2, g3)):
        full[0:outs, d * 256 : (d + 1) * 256] = g[...]
    full[outs : outs + 16, :] = low[...]
    full[outs + 16 : outs + 32, :] = high[...]
    rows[frames : frames + 16, :] = jnp.zeros((16, 128), F32)
    for pair in range(TAPS // 2):
        res = mul(full[...], weights[pair * 256 : (pair + 1) * 256, :], NT)
        for side in range(2):
            k = 2 * pair + side
            part = res[:, side * 128 : (side + 1) * 128]
            at = pl.ds(4 + k, outs, stride=STRIDE)
            if k < STRIDE:
                rows[at, :] = part[:outs]
                if k < 4:
                    rows[frames + 4 + k : frames + 5 + k, :] = part[outs + 16 : outs + 17]
            else:
                if k >= 12:
                    rows[k - 4 : k - 3, :] = rows[k - 4 : k - 3, :] + part[outs + 15 : outs + 16]
                rows[at, :] = rows[at, :] + part[:outs]
    step = 512
    for at in range(0, frames, step):
        out[at : at + step, :] = (
            rows[at + 8 : at + 8 + step, :] * factor[at : at + step, :]
        ).astype(BF)
    done[...] = jnp.zeros(done.shape, F32)


def input_grad(gs, low, high, weights, factor, after):
    frames, chans = factor.shape
    return call(
        input_grad_kernel,
        (shape((frames, chans)), TOKEN),
        [VMEM] * 9,
        "input_grad",
        [pltpu.VMEM((frames // STRIDE + 32, 1024), BF), pltpu.VMEM((frames + 16, chans), F32)],
        limit=24,
    )(*gs, low, high, weights, factor, after)


def total_kernel(own, a1, a2, a3, after, out):
    out[...] = (
        own[...] + a1[...].astype(F32) + a2[...].astype(F32) + a3[...].astype(F32)
    ).astype(BF)


def total(own, others, after):
    return call(total_kernel, shape((768, 256)), [VMEM] * 5, "total", limit=24)(
        own, *others, after
    )


def turn(value, axis, by):
    count = lax.axis_size(axis)
    return lax.ppermute(value, axis, [(i, (i + by) % count) for i in range(count)])


def beside(value, by):
    count = math.prod(lax.axis_size(a) for a in TM)
    pairs = [(i, i + by) for i in range(count) if 0 <= i + by < count]
    return lax.ppermute(value, TM, pairs)


def shards(features, snake_alpha, down_weight, grad_out):
    x, z, core, y = (lax.axis_index(a).astype(jnp.int32) for a in ("x", "z", "core", "chan"))

    gs = (
        grad_out,
        turn(grad_out, "chan", -1),
        turn(grad_out, "chan", 2),
        turn(grad_out, "chan", 1),
    )
    low, high = beside(features[-16:], 1), beside(features[:16], -1)

    at = jnp.stack([y, core])
    own, p1, p2, p3, done = weights(at, down_weight)
    near = (turn(p3, "chan", -1), turn(p2, "chan", 2), turn(p1, "chan", 1))
    taps, factor = prep(features, low, high, snake_alpha.reshape(1, -1), done)

    place = jnp.stack([core] + [(y + d) % 4 for d in range(4)])
    out = send(place, taps, gs)
    got = turn(out, "core", 1)
    kept, done = keep(place, taps, gs, got)
    arrived = lax.all_to_all(kept, "x", 0, 0)

    held = join(near, done)
    far = [turn(h, "core", 1) for h in held]
    mine, part1, part2, part3, full, first, last, done = encode(
        core.reshape(1), taps, own, gs, held, far
    )
    others = (turn(part1, "chan", 1), turn(part3, "chan", -1), turn(part2, "chan", 2))
    edges = beside(last, 1), beside(first, -1)
    summed, done = lines(arrived, done)
    spread = lax.all_to_all(summed, "z", 0, 0)
    grad_features, done = input_grad(gs, *edges, full, factor, done)

    encoded = total(mine, others, done)

    scale = 1.0 / math.sqrt(features.shape[0] // STRIDE * 64)
    down = jnp.sum(spread.astype(F32), axis=0) * scale
    grad_down = down.astype(BF).reshape(16, 16, 128)
    return (encoded, grad_features, grad_down)


def solution(mesh):
    tm, chan = mesh.shape["tm"], mesh.shape["chan"]
    fine = Mesh(mesh.devices.reshape(4, tm // 8, 2, chan), (*TM, "chan"))
    placed = (P(TM, "chan"), P("chan"), P(None, None, "chan"), P(TM, "chan"))
    return jax.shard_map(
        shards,
        mesh=fine,
        in_specs=placed,
        out_specs=(P(TM, "chan"), P(TM, "chan"), P(TM, None, "chan")),
        check_vma=False,
    )
```

```python
import functools
import math

import jax
import jax.numpy as jnp
from jax import lax
from jax.experimental import pallas as pl
from jax.experimental.pallas import tpu as pltpu
from jax.sharding import Mesh
from jax.sharding import PartitionSpec as P

STRIDE = 8
TAPS = 16
BF = jnp.bfloat16
F32 = jnp.float32
TM = ("x", "z", "core")
SIN = (1.0, -1.66666666e-01, 8.33333079e-03, -1.98408371e-04, 2.75240247e-06, -2.38669497e-08)
COS = (
    1.0,
    -0.5,
    4.16666665e-02,
    -1.38888838e-03,
    2.48010074e-05,
    -2.75233926e-07,
    1.98888297e-09,
)
PI_A = 3.140625
PI_B = math.pi - PI_A
VMEM = pl.BlockSpec(memory_space=pltpu.VMEM)
SMEM = pl.BlockSpec(memory_space=pltpu.SMEM)
HBM = pl.BlockSpec(memory_space=pltpu.HBM)
NN = (((1,), (0,)), ((), ()))
NT = (((1,), (1,)), ((), ()))


def mul(lhs, rhs, dims=NN):
    return lax.dot_general(lhs, rhs, dims, preferred_element_type=F32)


def call(kernel, outs, specs, name, scratch=(), limit=24, out_specs=None):
    return pl.pallas_call(
        kernel,
        out_shape=outs,
        in_specs=specs,
        out_specs=out_specs or jax.tree.map(lambda _: VMEM, outs),
        scratch_shapes=scratch,
        compiler_params=pltpu.CompilerParams(vmem_limit_bytes=limit * 2**20),
        cost_estimate=pl.CostEstimate(flops=int(TIME[name] * FACTOR * 1.15e9), bytes_accessed=1000, transcendentals=0),
        name=name,
    )


def shape(dims, dtype=BF):
    return jax.ShapeDtypeStruct(dims, dtype)


TOKEN = shape((8, 128), F32)


FACTOR = 1.1
TIME = dict(
    prep=7,
    weights=4,
    kernel_grad_send=3,
    kernel_grad_keep=4,
    join=1,
    total=1,
    encode=5,
    lines=1,
    input_grad=6,
)


def far_shape(dims, dtype=BF):
    return pltpu.HBM(dims, dtype)


def poly(coefs, z):
    out = z * coefs[-1] + coefs[-2]
    for c in coefs[-3::-1]:
        out = out * z + c
    return out


def sincos(theta):
    n = jnp.floor(theta * (1.0 / math.pi) + 0.5)
    r = (theta - n * PI_A) - n * PI_B
    z = r * r
    return r * poly(SIN, z), poly(COS, z)


def prep_kernel(feat, low, high, alpha, taps, factor, done, rows, held, sem):
    frames = feat.shape[0]
    a = alpha[...]
    inv = 1.0 / a

    def snake(values):
        wide = values.astype(F32)
        s, c = sincos(a * wide)
        return wide + s * s * inv, 1.0 + 2.0 * s * c

    rows[0:8, :] = snake(low[8:16, :])[0]
    rows[frames + 8 : frames + 16, :] = snake(high[0:8, :])[0]
    step, parts = 256, 4
    size = frames // parts
    copies = []
    for part in range(parts):

        def body(at, carry, part=part):
            here = pl.multiple_of(part * size + at * step, step)
            act, fac = snake(feat[pl.ds(here, step), :])
            rows[pl.ds(here + 8, step), :] = act
            held[pl.ds(here, step), :] = fac
            return carry

        lax.fori_loop(0, size // step, body, 0)
        lines = pl.ds(part * size, size)
        copies.append(pltpu.make_async_copy(held.at[lines], factor.at[lines], sem.at[part]))
        copies[-1].start()
    outs = frames // STRIDE
    for k in range(TAPS):
        taps[:, k * 128 : (k + 1) * 128] = rows[pl.ds(4 + k, outs, stride=STRIDE), :].astype(BF)
    done[...] = jnp.zeros(done.shape, F32)
    for c in copies:
        c.wait()


def prep(feat, low, high, alpha):
    frames, chans = feat.shape
    return call(
        prep_kernel,
        (shape((frames // STRIDE, TAPS * chans)), far_shape((frames, chans), F32), TOKEN),
        [VMEM] * 4,
        "prep",
        [
            pltpu.VMEM((frames + 16, chans), F32),
            pltpu.VMEM((frames, chans), F32),
            pltpu.SemaphoreType.DMA((4,)),
        ],
        out_specs=(VMEM, HBM, VMEM),
    )(feat, low, high, alpha)


def weights_kernel(
    place, whole, after, own, p1, p2, p3, done, buf, rows, held, sem, out_sem
):
    y, core = place[0], place[1]
    copies = [
        pltpu.make_async_copy(
            whole.at[pl.ds(pl.multiple_of(lax.rem(y + s, 4) * 128, 128), 128)], buf.at[s], sem.at[s]
        )
        for s in range(4)
    ]
    for c in copies:
        c.start()
    for s, out in ((0, held), (1, p1), (3, p3), (2, p2)):
        copies[s].wait()
        count = TAPS if s == 0 else TAPS // 2
        for h in range(2):
            lanes = slice(h * 128, h * 128 + 128)
            rows[...] = buf[s, :, :, lanes].astype(F32).reshape(128 * TAPS, 128)
            for k in range(count):
                tap = k if s == 0 else TAPS // 2 * core + k
                out[k * 128 : (k + 1) * 128, lanes] = rows[
                    pl.ds(tap, 128, stride=TAPS), :
                ].astype(BF)
        if s == 0:
            sent = pltpu.make_async_copy(held, own, out_sem)
            sent.start()
    sent.wait()
    done[...] = jnp.zeros(done.shape, F32)


def weights(place, whole, after):
    return call(
        weights_kernel,
        (far_shape((2048, 256)),) + (shape((1024, 256)),) * 3 + (TOKEN,),
        [SMEM, HBM, VMEM],
        "weights",
        [
            pltpu.VMEM((4, 128, TAPS, 256), BF),
            pltpu.VMEM((128 * TAPS, 128), F32),
            pltpu.VMEM((2048, 256), BF),
            pltpu.SemaphoreType.DMA((4,)),
            pltpu.SemaphoreType.DMA,
        ],
        out_specs=(HBM,) + (VMEM,) * 4,
    )(place, whole, after)


def choose(gs, which, order, lhs):
    row = lax.broadcasted_iota(jnp.int32, (128, 256), 0)
    col = lax.broadcasted_iota(jnp.int32, (128, 256), 1)
    want = (row // 16) * 32 + which * 16 + row % 16
    pick = jnp.where(col == want, 1.0, 0.0).astype(BF)
    for d, g in enumerate(gs):
        at = pl.multiple_of(order[d] * 128, 128)
        lhs[pl.ds(at, 128), :] = mul(pick, g[...], NT).astype(BF)


def send_kernel(place, taps, g0, g1, g2, g3, after, out, lhs):
    choose((g0, g1, g2, g3), 1 - place[0], [place[1 + d] for d in range(4)], lhs)
    for n in range(0, 2048, 256):
        out[:, n : n + 256] = mul(lhs[...], taps[:, n : n + 256]).astype(BF)


def send(place, taps, gs, after):
    return call(
        send_kernel,
        shape((512, 2048)),
        [SMEM] + [VMEM] * 6,
        "kernel_grad_send",
        [pltpu.VMEM((512, 768), BF)],
        limit=24,
    )(place, taps, *gs, after)


def keep_kernel(place, taps, g0, g1, g2, g3, got, out, first, last, done, lhs, held, ends, sem):
    choose((g0, g1, g2, g3), place[0], [place[1 + d] for d in range(4)], lhs)
    for d, g in enumerate((g0, g1, g2, g3)):
        ends[0, :, d * 256 : (d + 1) * 256] = g[0:16, :]
        ends[1, :, d * 256 : (d + 1) * 256] = g[752:768, :]
    copies = [
        pltpu.make_async_copy(ends.at[0], first, sem.at[4]),
        pltpu.make_async_copy(ends.at[1], last, sem.at[5]),
    ]
    for c in copies:
        c.start()
    for n in range(0, 2048, 512):
        cols = slice(n, n + 512)
        both = mul(lhs[...], taps[:, cols]) + got[:, cols].astype(F32)
        for to in range(4):
            held[to, :, cols] = both[to * 128 : (to + 1) * 128].astype(BF)
        copies.append(
            pltpu.make_async_copy(held.at[:, :, cols], out.at[:, :, cols], sem.at[n // 512])
        )
        copies[-1].start()
    done[...] = jnp.zeros(done.shape, F32)
    for c in copies:
        c.wait()


def keep(place, taps, gs, got):
    return call(
        keep_kernel,
        (far_shape((4, 128, 2048)),) + (far_shape((16, 1024)),) * 2 + (TOKEN,),
        [SMEM] + [VMEM] * 6,
        "kernel_grad_keep",
        [
            pltpu.VMEM((512, 768), BF),
            pltpu.VMEM((4, 128, 2048), BF),
            pltpu.VMEM((2, 16, 1024), BF),
            pltpu.SemaphoreType.DMA((6,)),
        ],
        out_specs=(HBM,) * 3 + (VMEM,),
        limit=24,
    )(place, taps, *gs, got)


def join_kernel(a1, a2, a3, low, high, after, o1, o2, o3):
    for a, out in ((a1, o1), (a2, o2), (a3, o3)):
        out[...] = a[...]


def join(near, edges, after):
    return call(join_kernel, (shape((1024, 256)),) * 3, [VMEM] * 6, "join", limit=24)(*near, *edges, after)


def encode_kernel(
    core, taps, own, a1, a2, a3, b1, b2, b3, o0, o1, o2, o3, full, done, held, mine, theirs, sem
):
    here = pl.multiple_of(core[0] * 1024, 1024)
    there = pl.multiple_of(1024 - core[0] * 1024, 1024)
    first = pltpu.make_async_copy(own, held.at[:, 0:256], sem.at[0])
    first.start()
    for d, (a, b) in enumerate(((a1, b1), (a2, b2), (a3, b3))):
        cols = slice(256 * (d + 1), 256 * (d + 2))
        held[pl.ds(here, 1024), cols] = a[...]
        held[pl.ds(there, 1024), cols] = b[...]
    first.wait()
    copies = [pltpu.make_async_copy(held, full, sem.at[1])]
    copies[0].start()
    for d, out in ((0, o0), (1, o1), (3, o3), (2, o2)):
        value = mul(taps[...], held[:, d * 256 : (d + 1) * 256])
        if d == 0:
            mine[...] = value
            copies.append(pltpu.make_async_copy(mine, out, sem.at[2]))
        else:
            theirs[d - 1] = value.astype(BF)
            copies.append(pltpu.make_async_copy(theirs.at[d - 1], out, sem.at[2 + d]))
        copies[-1].start()
    done[...] = jnp.zeros(done.shape, F32)
    for c in copies:
        c.wait()


def encode(core, taps, own, near, far):
    return call(
        encode_kernel,
        (far_shape((768, 256), F32),)
        + (far_shape((768, 256)),) * 3
        + (far_shape((2048, 1024)), TOKEN),
        [SMEM, VMEM, HBM] + [VMEM] * 6,
        "encode",
        [
            pltpu.VMEM((2048, 1024), BF),
            pltpu.VMEM((768, 256), F32),
            pltpu.VMEM((3, 768, 256), BF),
            pltpu.SemaphoreType.DMA((6,)),
        ],
        out_specs=(HBM,) * 5 + (VMEM,),
    )(core, taps, own, *near, *far)


def lines_kernel(parts, after, out, done):
    for m in range(8):
        here = slice(m * 16, m * 16 + 16)
        out[m] = sum(parts[n, here, :].astype(F32) for n in range(4)).astype(BF)
    done[...] = jnp.zeros(done.shape, F32)


def lines(parts, after):
    return call(lines_kernel, (shape((8, 16, 2048)), TOKEN), [VMEM] * 2, "lines", limit=24)(
        parts, after
    )


def input_grad_kernel(g0, g1, g2, g3, low, high, weights, factor, after, out, done, full, rows):
    outs = g0.shape[0]
    frames = out.shape[0]
    for d, g in enumerate((g0, g1, g2, g3)):
        full[0:outs, d * 256 : (d + 1) * 256] = g[...]
    full[outs : outs + 16, :] = low[...]
    full[outs + 16 : outs + 32, :] = high[...]
    rows[frames : frames + 16, :] = jnp.zeros((16, 128), F32)
    for pair in range(TAPS // 2):
        res = mul(full[...], weights[pair * 256 : (pair + 1) * 256, :], NT)
        for side in range(2):
            k = 2 * pair + side
            part = res[:, side * 128 : (side + 1) * 128]
            at = pl.ds(4 + k, outs, stride=STRIDE)
            if k < STRIDE:
                rows[at, :] = part[:outs]
                if k < 4:
                    rows[frames + 4 + k : frames + 5 + k, :] = part[outs + 16 : outs + 17]
            else:
                if k >= 12:
                    rows[k - 4 : k - 3, :] = rows[k - 4 : k - 3, :] + part[outs + 15 : outs + 16]
                rows[at, :] = rows[at, :] + part[:outs]
    step = 512
    for at in range(0, frames, step):
        out[at : at + step, :] = (
            rows[at + 8 : at + 8 + step, :] * factor[at : at + step, :]
        ).astype(BF)
    done[...] = jnp.zeros(done.shape, F32)


def input_grad(gs, low, high, weights, factor, after):
    frames, chans = factor.shape
    return call(
        input_grad_kernel,
        (shape((frames, chans)), TOKEN),
        [VMEM] * 9,
        "input_grad",
        [pltpu.VMEM((frames // STRIDE + 32, 1024), BF), pltpu.VMEM((frames + 16, chans), F32)],
        limit=24,
    )(*gs, low, high, weights, factor, after)


def total_kernel(own, a1, a2, a3, after, out):
    out[...] = (
        own[...] + a1[...].astype(F32) + a2[...].astype(F32) + a3[...].astype(F32)
    ).astype(BF)


def total(own, others, after):
    return call(total_kernel, shape((768, 256)), [VMEM] * 5, "total", limit=24)(
        own, *others, after
    )


def turn(value, axis, by):
    count = lax.axis_size(axis)
    return lax.ppermute(value, axis, [(i, (i + by) % count) for i in range(count)])


def beside(value, by):
    count = math.prod(lax.axis_size(a) for a in TM)
    pairs = [(i, i + by) for i in range(count) if 0 <= i + by < count]
    return lax.ppermute(value, TM, pairs)


def shards(features, snake_alpha, down_weight, grad_out):
    x, z, core, y = (lax.axis_index(a).astype(jnp.int32) for a in ("x", "z", "core", "chan"))

    gs = (
        grad_out,
        turn(grad_out, "chan", -1),
        turn(grad_out, "chan", 2),
        turn(grad_out, "chan", 1),
    )
    low, high = beside(features[-16:], 1), beside(features[:16], -1)

    at = jnp.stack([y, core])
    taps, factor, done = prep(features, low, high, snake_alpha.reshape(1, -1))
    own, p1, p2, p3, done = weights(at, down_weight, done)
    near = (turn(p3, "chan", -1), turn(p2, "chan", 2), turn(p1, "chan", 1))

    place = jnp.stack([core] + [(y + d) % 4 for d in range(4)])
    out = send(place, taps, gs, done)
    got = turn(out, "core", 1)
    kept, first, last, done = keep(place, taps, gs, got)
    edges = beside(last, 1), beside(first, -1)
    arrived = lax.all_to_all(kept, "x", 0, 0)

    held = join(near, edges, done)
    far = [turn(h, "core", 1) for h in held]
    mine, part1, part2, part3, full, done = encode(
        core.reshape(1), taps, own, held, far
    )
    others = (turn(part1, "chan", 1), turn(part3, "chan", -1), turn(part2, "chan", 2))
    summed, done = lines(arrived, done)
    spread = lax.all_to_all(summed, "z", 0, 0)
    grad_features, done = input_grad(gs, *edges, full, factor, done)

    encoded = total(mine, others, done)

    scale = 1.0 / math.sqrt(features.shape[0] // STRIDE * 64)
    down = jnp.sum(spread.astype(F32), axis=0) * scale
    grad_down = down.astype(BF).reshape(16, 16, 128)
    return (encoded, grad_features, grad_down)


def solution(mesh):
    tm, chan = mesh.shape["tm"], mesh.shape["chan"]
    fine = Mesh(mesh.devices.reshape(4, tm // 8, 2, chan), (*TM, "chan"))
    placed = (P(TM, "chan"), P("chan"), P(None, None, "chan"), P(TM, "chan"))
    return jax.shard_map(
        shards,
        mesh=fine,
        in_specs=placed,
        out_specs=(P(TM, "chan"), P(TM, "chan"), P(TM, None, "chan")),
        check_vma=False,
    )
```

```python
import functools
import math

import jax
import jax.numpy as jnp
from jax import lax
from jax.experimental import pallas as pl
from jax.experimental.pallas import tpu as pltpu
from jax.sharding import Mesh
from jax.sharding import PartitionSpec as P

STRIDE = 8
TAPS = 16
BF = jnp.bfloat16
F32 = jnp.float32
TM = ("x", "z", "core")
SIN = (1.0, -1.66666666e-01, 8.33333079e-03, -1.98408371e-04, 2.75240247e-06, -2.38669497e-08)
COS = (
    1.0,
    -0.5,
    4.16666665e-02,
    -1.38888838e-03,
    2.48010074e-05,
    -2.75233926e-07,
    1.98888297e-09,
)
PI_A = 3.140625
PI_B = math.pi - PI_A
VMEM = pl.BlockSpec(memory_space=pltpu.VMEM)
SMEM = pl.BlockSpec(memory_space=pltpu.SMEM)
ANY = pl.BlockSpec(memory_space=pl.ANY)
HBM = pl.BlockSpec(memory_space=pltpu.HBM)
NN = (((1,), (0,)), ((), ()))
NT = (((1,), (1,)), ((), ()))


def mul(lhs, rhs, dims=NN):
    return lax.dot_general(lhs, rhs, dims, preferred_element_type=F32)


def call(kernel, outs, specs, name, scratch=(), limit=24, out_specs=None, aliases=None):
    return pl.pallas_call(
        kernel,
        out_shape=outs,
        in_specs=specs,
        out_specs=out_specs or jax.tree.map(lambda _: VMEM, outs),
        scratch_shapes=scratch,
        compiler_params=pltpu.CompilerParams(vmem_limit_bytes=limit * 2**20),
        cost_estimate=pl.CostEstimate(flops=int(TIME[name] * FACTOR * 1.15e9), bytes_accessed=1000, transcendentals=0),
        name=name,
        input_output_aliases=aliases or {},
    )


def shape(dims, dtype=BF):
    return jax.ShapeDtypeStruct(dims, dtype)


TOKEN = shape((8, 128), F32)


FACTOR = 1.1
TIME = dict(
    prep=7,
    weights=4,
    kernel_grad_send=3,
    kernel_grad_keep=4,
    join=1,
    total=1,
    encode=5,
    lines=1,
    input_grad=6,
)


def far_shape(dims, dtype=BF):
    return pltpu.HBM(dims, dtype)


def poly(coefs, z):
    out = z * coefs[-1] + coefs[-2]
    for c in coefs[-3::-1]:
        out = out * z + c
    return out


def sincos(theta):
    n = jnp.floor(theta * (1.0 / math.pi) + 0.5)
    r = (theta - n * PI_A) - n * PI_B
    z = r * r
    return r * poly(SIN, z), poly(COS, z)


def prep_kernel(feat, low, high, alpha, after, taps, factor, rows, held, sem):
    frames = feat.shape[0]
    a = alpha[...]
    inv = 1.0 / a

    def snake(values):
        wide = values.astype(F32)
        s, c = sincos(a * wide)
        return wide + s * s * inv, 1.0 + 2.0 * s * c

    rows[0:8, :] = snake(low[8:16, :])[0]
    rows[frames + 8 : frames + 16, :] = snake(high[0:8, :])[0]
    step, parts = 256, 4
    size = frames // parts
    copies = []
    for part in range(parts):

        def body(at, carry, part=part):
            here = pl.multiple_of(part * size + at * step, step)
            act, fac = snake(feat[pl.ds(here, step), :])
            rows[pl.ds(here + 8, step), :] = act
            held[pl.ds(here, step), :] = fac
            return carry

        lax.fori_loop(0, size // step, body, 0)
        lines = pl.ds(part * size, size)
        copies.append(pltpu.make_async_copy(held.at[lines], factor.at[lines], sem.at[part]))
        copies[-1].start()
    outs = frames // STRIDE
    for k in range(TAPS):
        taps[:, k * 128 : (k + 1) * 128] = rows[pl.ds(4 + k, outs, stride=STRIDE), :].astype(BF)
    for c in copies:
        c.wait()


def prep(feat, low, high, alpha, after):
    frames, chans = feat.shape
    return call(
        prep_kernel,
        (shape((frames // STRIDE, TAPS * chans)), far_shape((frames, chans), F32)),
        [VMEM] * 5,
        "prep",
        [
            pltpu.VMEM((frames + 16, chans), F32),
            pltpu.VMEM((frames, chans), F32),
            pltpu.SemaphoreType.DMA((4,)),
        ],
        out_specs=(VMEM, HBM),
    )(feat, low, high, alpha, after)


def weights_kernel(
    place, whole, own, p1, p2, p3, done, buf, rows, held, sem, out_sem
):
    y, core = place[0], place[1]
    copies = [
        pltpu.make_async_copy(
            whole.at[pl.ds(pl.multiple_of(lax.rem(y + s, 4) * 128, 128), 128)], buf.at[s], sem.at[s]
        )
        for s in range(4)
    ]
    for c in copies:
        c.start()
    for s, out in ((0, held), (1, p1), (3, p3), (2, p2)):
        copies[s].wait()
        count = TAPS if s == 0 else TAPS // 2
        for h in range(2):
            lanes = slice(h * 128, h * 128 + 128)
            rows[...] = buf[s, :, :, lanes].astype(F32).reshape(128 * TAPS, 128)
            for k in range(count):
                tap = k if s == 0 else TAPS // 2 * core + k
                out[k * 128 : (k + 1) * 128, lanes] = rows[
                    pl.ds(tap, 128, stride=TAPS), :
                ].astype(BF)
        if s == 0:
            sent = pltpu.make_async_copy(held, own, out_sem)
            sent.start()
    sent.wait()
    done[...] = jnp.zeros(done.shape, F32)


def weights(place, whole):
    return call(
        weights_kernel,
        (far_shape((2048, 256)),) + (shape((1024, 256)),) * 3 + (TOKEN,),
        [SMEM, HBM],
        "weights",
        [
            pltpu.VMEM((4, 128, TAPS, 256), BF),
            pltpu.VMEM((128 * TAPS, 128), F32),
            pltpu.VMEM((2048, 256), BF),
            pltpu.SemaphoreType.DMA((4,)),
            pltpu.SemaphoreType.DMA,
        ],
        out_specs=(HBM,) + (VMEM,) * 4,
    )(place, whole)


def choose(gs, which, order, lhs):
    row = lax.broadcasted_iota(jnp.int32, (128, 256), 0)
    col = lax.broadcasted_iota(jnp.int32, (128, 256), 1)
    want = (row // 16) * 32 + which * 16 + row % 16
    pick = jnp.where(col == want, 1.0, 0.0).astype(BF)
    for d, g in enumerate(gs):
        at = pl.multiple_of(order[d] * 128, 128)
        lhs[pl.ds(at, 128), :] = mul(pick, g[...], NT).astype(BF)


def send_kernel(place, taps, g0, g1, g2, g3, out, lhs):
    choose((g0, g1, g2, g3), 1 - place[0], [place[1 + d] for d in range(4)], lhs)
    for n in range(0, 2048, 256):
        out[:, n : n + 256] = mul(lhs[...], taps[:, n : n + 256]).astype(BF)


def send(place, taps, gs):
    return call(
        send_kernel,
        shape((512, 2048)),
        [SMEM] + [VMEM] * 5,
        "kernel_grad_send",
        [pltpu.VMEM((512, 768), BF)],
        limit=24,
    )(place, taps, *gs)


def keep_kernel(place, taps, g0, g1, g2, g3, got, out, first, last, done, lhs, held, ends, sem):
    choose((g0, g1, g2, g3), place[0], [place[1 + d] for d in range(4)], lhs)
    for d, g in enumerate((g0, g1, g2, g3)):
        ends[0, :, d * 256 : (d + 1) * 256] = g[0:16, :]
        ends[1, :, d * 256 : (d + 1) * 256] = g[752:768, :]
    copies = [
        pltpu.make_async_copy(ends.at[0], first, sem.at[4]),
        pltpu.make_async_copy(ends.at[1], last, sem.at[5]),
    ]
    for c in copies:
        c.start()
    for n in range(0, 2048, 512):
        cols = slice(n, n + 512)
        both = mul(lhs[...], taps[:, cols]) + got[:, cols].astype(F32)
        for to in range(4):
            held[to, :, cols] = both[to * 128 : (to + 1) * 128].astype(BF)
        copies.append(
            pltpu.make_async_copy(held.at[:, :, cols], out.at[:, :, cols], sem.at[n // 512])
        )
        copies[-1].start()
    done[...] = jnp.zeros(done.shape, F32)
    for c in copies:
        c.wait()


def keep(place, taps, gs, got):
    return call(
        keep_kernel,
        (far_shape((4, 128, 2048)),) + (far_shape((16, 1024)),) * 2 + (TOKEN,),
        [SMEM] + [VMEM] * 6,
        "kernel_grad_keep",
        [
            pltpu.VMEM((512, 768), BF),
            pltpu.VMEM((4, 128, 2048), BF),
            pltpu.VMEM((2, 16, 1024), BF),
            pltpu.SemaphoreType.DMA((6,)),
        ],
        out_specs=(HBM,) * 3 + (VMEM,),
        limit=24,
    )(place, taps, *gs, got)


def join_kernel(*refs):
    del refs


def join(near, edges, after):
    return call(
        join_kernel,
        (shape((1024, 256)),) * 3,
        [ANY] * 6,
        "join",
        out_specs=(ANY,) * 3,
        aliases={0: 0, 1: 1, 2: 2},
    )(*near, *edges, after)


def encode_kernel(
    core, taps, own, a1, a2, a3, b1, b2, b3, o0, o1, o2, o3, full, done, held, mine, theirs, sem
):
    here = pl.multiple_of(core[0] * 1024, 1024)
    there = pl.multiple_of(1024 - core[0] * 1024, 1024)
    first = pltpu.make_async_copy(own, held.at[:, 0:256], sem.at[0])
    first.start()
    for d, (a, b) in enumerate(((a1, b1), (a2, b2), (a3, b3))):
        cols = slice(256 * (d + 1), 256 * (d + 2))
        held[pl.ds(here, 1024), cols] = a[...]
        held[pl.ds(there, 1024), cols] = b[...]
    first.wait()
    copies = [pltpu.make_async_copy(held, full, sem.at[1])]
    copies[0].start()
    for d, out in ((0, o0), (1, o1), (3, o3), (2, o2)):
        value = mul(taps[...], held[:, d * 256 : (d + 1) * 256])
        if d == 0:
            mine[...] = value
            copies.append(pltpu.make_async_copy(mine, out, sem.at[2]))
        else:
            theirs[d - 1] = value.astype(BF)
            copies.append(pltpu.make_async_copy(theirs.at[d - 1], out, sem.at[2 + d]))
        copies[-1].start()
    done[...] = jnp.zeros(done.shape, F32)
    for c in copies:
        c.wait()


def encode(core, taps, own, near, far):
    return call(
        encode_kernel,
        (far_shape((768, 256), F32),)
        + (far_shape((768, 256)),) * 3
        + (far_shape((2048, 1024)), TOKEN),
        [SMEM, VMEM, HBM] + [VMEM] * 6,
        "encode",
        [
            pltpu.VMEM((2048, 1024), BF),
            pltpu.VMEM((768, 256), F32),
            pltpu.VMEM((3, 768, 256), BF),
            pltpu.SemaphoreType.DMA((6,)),
        ],
        out_specs=(HBM,) * 5 + (VMEM,),
    )(core, taps, own, *near, *far)


def lines_kernel(parts, after, out, done):
    for m in range(8):
        here = slice(m * 16, m * 16 + 16)
        out[m] = sum(parts[n, here, :].astype(F32) for n in range(4)).astype(BF)
    done[...] = jnp.zeros(done.shape, F32)


def lines(parts, after):
    return call(lines_kernel, (shape((8, 16, 2048)), TOKEN), [VMEM] * 2, "lines", limit=24)(
        parts, after
    )


def input_grad_kernel(g0, g1, g2, g3, low, high, weights, factor, after, out, done, full, rows):
    outs = g0.shape[0]
    frames = out.shape[0]
    for d, g in enumerate((g0, g1, g2, g3)):
        full[0:outs, d * 256 : (d + 1) * 256] = g[...]
    full[outs : outs + 16, :] = low[...]
    full[outs + 16 : outs + 32, :] = high[...]
    rows[frames : frames + 16, :] = jnp.zeros((16, 128), F32)
    for pair in range(TAPS // 2):
        res = mul(full[...], weights[pair * 256 : (pair + 1) * 256, :], NT)
        for side in range(2):
            k = 2 * pair + side
            part = res[:, side * 128 : (side + 1) * 128]
            at = pl.ds(4 + k, outs, stride=STRIDE)
            if k < STRIDE:
                rows[at, :] = part[:outs]
                if k < 4:
                    rows[frames + 4 + k : frames + 5 + k, :] = part[outs + 16 : outs + 17]
            else:
                if k >= 12:
                    rows[k - 4 : k - 3, :] = rows[k - 4 : k - 3, :] + part[outs + 15 : outs + 16]
                rows[at, :] = rows[at, :] + part[:outs]
    step = 512
    for at in range(0, frames, step):
        out[at : at + step, :] = (
            rows[at + 8 : at + 8 + step, :] * factor[at : at + step, :]
        ).astype(BF)
    done[...] = jnp.zeros(done.shape, F32)


def input_grad(gs, low, high, weights, factor, after):
    frames, chans = factor.shape
    return call(
        input_grad_kernel,
        (shape((frames, chans)), TOKEN),
        [VMEM] * 9,
        "input_grad",
        [pltpu.VMEM((frames // STRIDE + 32, 1024), BF), pltpu.VMEM((frames + 16, chans), F32)],
        limit=24,
    )(*gs, low, high, weights, factor, after)


def total_kernel(own, a1, a2, a3, after, out):
    out[...] = (
        own[...] + a1[...].astype(F32) + a2[...].astype(F32) + a3[...].astype(F32)
    ).astype(BF)


def total(own, others, after):
    return call(total_kernel, shape((768, 256)), [VMEM] * 5, "total", limit=24)(
        own, *others, after
    )


def turn(value, axis, by):
    count = lax.axis_size(axis)
    return lax.ppermute(value, axis, [(i, (i + by) % count) for i in range(count)])


def beside(value, by):
    count = math.prod(lax.axis_size(a) for a in TM)
    pairs = [(i, i + by) for i in range(count) if 0 <= i + by < count]
    return lax.ppermute(value, TM, pairs)


def shards(features, snake_alpha, down_weight, grad_out):
    x, z, core, y = (lax.axis_index(a).astype(jnp.int32) for a in ("x", "z", "core", "chan"))

    gs = (
        grad_out,
        turn(grad_out, "chan", -1),
        turn(grad_out, "chan", 2),
        turn(grad_out, "chan", 1),
    )
    low, high = beside(features[-16:], 1), beside(features[:16], -1)

    at = jnp.stack([y, core])
    own, p1, p2, p3, done = weights(at, down_weight)
    taps, factor = prep(features, low, high, snake_alpha.reshape(1, -1), done)
    near = (turn(p3, "chan", -1), turn(p2, "chan", 2), turn(p1, "chan", 1))

    place = jnp.stack([core] + [(y + d) % 4 for d in range(4)])
    out = send(place, taps, gs)
    got = turn(out, "core", 1)
    kept, first, last, done = keep(place, taps, gs, got)
    edges = beside(last, 1), beside(first, -1)
    arrived = lax.all_to_all(kept, "x", 0, 0)

    held = join(near, edges, done)
    far = [turn(h, "core", 1) for h in held]
    mine, part1, part2, part3, full, done = encode(
        core.reshape(1), taps, own, held, far
    )
    others = (turn(part1, "chan", 1), turn(part3, "chan", -1), turn(part2, "chan", 2))
    summed, done = lines(arrived, done)
    spread = lax.all_to_all(summed, "z", 0, 0)
    grad_features, done = input_grad(gs, *edges, full, factor, done)

    encoded = total(mine, others, done)

    scale = 1.0 / math.sqrt(features.shape[0] // STRIDE * 64)
    down = jnp.sum(spread.astype(F32), axis=0) * scale
    grad_down = down.astype(BF).reshape(16, 16, 128)
    return (encoded, grad_features, grad_down)


def solution(mesh):
    tm, chan = mesh.shape["tm"], mesh.shape["chan"]
    fine = Mesh(mesh.devices.reshape(4, tm // 8, 2, chan), (*TM, "chan"))
    placed = (P(TM, "chan"), P("chan"), P(None, None, "chan"), P(TM, "chan"))
    return jax.shard_map(
        shards,
        mesh=fine,
        in_specs=placed,
        out_specs=(P(TM, "chan"), P(TM, "chan"), P(TM, None, "chan")),
        check_vma=False,
    )
```

```python
import functools
import math

import jax
import jax.numpy as jnp
from jax import lax
from jax.experimental import pallas as pl
from jax.experimental.pallas import tpu as pltpu
from jax.sharding import Mesh
from jax.sharding import PartitionSpec as P

STRIDE = 8
TAPS = 16
BF = jnp.bfloat16
F32 = jnp.float32
TM = ("x", "z", "core")
SIN = (1.0, -1.66666666e-01, 8.33333079e-03, -1.98408371e-04, 2.75240247e-06, -2.38669497e-08)
COS = (
    1.0,
    -0.5,
    4.16666665e-02,
    -1.38888838e-03,
    2.48010074e-05,
    -2.75233926e-07,
    1.98888297e-09,
)
PI_A = 3.140625
PI_B = math.pi - PI_A
VMEM = pl.BlockSpec(memory_space=pltpu.VMEM)
SMEM = pl.BlockSpec(memory_space=pltpu.SMEM)
ANY = pl.BlockSpec(memory_space=pl.ANY)
HBM = pl.BlockSpec(memory_space=pltpu.HBM)
NN = (((1,), (0,)), ((), ()))
NT = (((1,), (1,)), ((), ()))


def mul(lhs, rhs, dims=NN):
    return lax.dot_general(lhs, rhs, dims, preferred_element_type=F32)


def call(kernel, outs, specs, name, scratch=(), limit=24, out_specs=None, aliases=None):
    return pl.pallas_call(
        kernel,
        out_shape=outs,
        in_specs=specs,
        out_specs=out_specs or jax.tree.map(lambda _: VMEM, outs),
        scratch_shapes=scratch,
        compiler_params=pltpu.CompilerParams(vmem_limit_bytes=limit * 2**20),
        cost_estimate=pl.CostEstimate(flops=int(TIME[name] * FACTOR * 1.15e9), bytes_accessed=1000, transcendentals=0),
        name=name,
        input_output_aliases=aliases or {},
    )


def shape(dims, dtype=BF):
    return jax.ShapeDtypeStruct(dims, dtype)


TOKEN = shape((8, 128), F32)


FACTOR = 1.1
TIME = dict(
    prep=2,
    weights=1,
    kernel_grad_send=3,
    kernel_grad_keep=4,
    join=1,
    total=1,
    encode=5,
    lines=1,
    input_grad=6,
)


def far_shape(dims, dtype=BF):
    return pltpu.HBM(dims, dtype)


def poly(coefs, z):
    out = z * coefs[-1] + coefs[-2]
    for c in coefs[-3::-1]:
        out = out * z + c
    return out


def sincos(theta):
    n = jnp.floor(theta * (1.0 / math.pi) + 0.5)
    r = (theta - n * PI_A) - n * PI_B
    z = r * r
    return r * poly(SIN, z), poly(COS, z)


def prep_kernel(feat, low, high, alpha, after, taps, factor, rows, held, sem):
    frames = feat.shape[0]
    a = alpha[...]
    inv = 1.0 / a

    def snake(values):
        wide = values.astype(F32)
        s, c = sincos(a * wide)
        return wide + s * s * inv, 1.0 + 2.0 * s * c

    rows[0:8, :] = snake(low[8:16, :])[0]
    rows[frames + 8 : frames + 16, :] = snake(high[0:8, :])[0]
    step, parts = 256, 4
    size = frames // parts
    copies = []
    for part in range(parts):

        def body(at, carry, part=part):
            here = pl.multiple_of(part * size + at * step, step)
            act, fac = snake(feat[pl.ds(here, step), :])
            rows[pl.ds(here + 8, step), :] = act
            held[pl.ds(here, step), :] = fac
            return carry

        lax.fori_loop(0, size // step, body, 0)
        lines = pl.ds(part * size, size)
        copies.append(pltpu.make_async_copy(held.at[lines], factor.at[lines], sem.at[part]))
        copies[-1].start()
    outs = frames // STRIDE
    for k in range(TAPS):
        taps[:, k * 128 : (k + 1) * 128] = rows[pl.ds(4 + k, outs, stride=STRIDE), :].astype(BF)
    for c in copies:
        c.wait()


def prep(feat, low, high, alpha, after):
    frames, chans = feat.shape
    return call(
        prep_kernel,
        (shape((frames // STRIDE, TAPS * chans)), far_shape((frames, chans), F32)),
        [VMEM] * 5,
        "prep",
        [
            pltpu.VMEM((frames + 16, chans), F32),
            pltpu.VMEM((frames, chans), F32),
            pltpu.SemaphoreType.DMA((4,)),
        ],
        out_specs=(VMEM, HBM),
    )(feat, low, high, alpha, after)


def weights_kernel(
    place, whole, head, tail, own, p1, p2, p3, o_head, o_tail, done, buf, rows, held, sem, out_sem
):
    y, core = place[0], place[1]
    copies = [
        pltpu.make_async_copy(
            whole.at[pl.ds(pl.multiple_of(lax.rem(y + s, 4) * 128, 128), 128)], buf.at[s], sem.at[s]
        )
        for s in range(4)
    ]
    for c in copies:
        c.start()
    for s, out in ((0, held), (1, p1), (3, p3), (2, p2)):
        copies[s].wait()
        count = TAPS if s == 0 else TAPS // 2
        for h in range(2):
            lanes = slice(h * 128, h * 128 + 128)
            rows[...] = buf[s, :, :, lanes].astype(F32).reshape(128 * TAPS, 128)
            for k in range(count):
                tap = k if s == 0 else TAPS // 2 * core + k
                out[k * 128 : (k + 1) * 128, lanes] = rows[
                    pl.ds(tap, 128, stride=TAPS), :
                ].astype(BF)
        if s == 0:
            sent = pltpu.make_async_copy(held, own, out_sem)
            sent.start()
    o_head[...] = head[...]
    o_tail[...] = tail[...]
    sent.wait()
    done[...] = jnp.zeros(done.shape, F32)


def weights(place, whole, head, tail):
    return call(
        weights_kernel,
        (far_shape((2048, 256)),) + (shape((1024, 256)),) * 3 + (shape((16, 128)),) * 2 + (TOKEN,),
        [SMEM, HBM, VMEM, VMEM],
        "weights",
        [
            pltpu.VMEM((4, 128, TAPS, 256), BF),
            pltpu.VMEM((128 * TAPS, 128), F32),
            pltpu.VMEM((2048, 256), BF),
            pltpu.SemaphoreType.DMA((4,)),
            pltpu.SemaphoreType.DMA,
        ],
        out_specs=(HBM,) + (VMEM,) * 6,
    )(place, whole, head, tail)


def choose(gs, which, order, lhs):
    row = lax.broadcasted_iota(jnp.int32, (128, 256), 0)
    col = lax.broadcasted_iota(jnp.int32, (128, 256), 1)
    want = (row // 16) * 32 + which * 16 + row % 16
    pick = jnp.where(col == want, 1.0, 0.0).astype(BF)
    for d, g in enumerate(gs):
        at = pl.multiple_of(order[d] * 128, 128)
        lhs[pl.ds(at, 128), :] = mul(pick, g[...], NT).astype(BF)


def send_kernel(place, taps, g0, g1, g2, g3, out, lhs):
    choose((g0, g1, g2, g3), 1 - place[0], [place[1 + d] for d in range(4)], lhs)
    for n in range(0, 2048, 256):
        out[:, n : n + 256] = mul(lhs[...], taps[:, n : n + 256]).astype(BF)


def send(place, taps, gs):
    return call(
        send_kernel,
        shape((512, 2048)),
        [SMEM] + [VMEM] * 5,
        "kernel_grad_send",
        [pltpu.VMEM((512, 768), BF)],
        limit=24,
    )(place, taps, *gs)


def keep_kernel(place, taps, g0, g1, g2, g3, got, out, first, last, done, lhs, held, ends, sem):
    choose((g0, g1, g2, g3), place[0], [place[1 + d] for d in range(4)], lhs)
    for d, g in enumerate((g0, g1, g2, g3)):
        ends[0, :, d * 256 : (d + 1) * 256] = g[0:16, :]
        ends[1, :, d * 256 : (d + 1) * 256] = g[752:768, :]
    copies = [
        pltpu.make_async_copy(ends.at[0], first, sem.at[4]),
        pltpu.make_async_copy(ends.at[1], last, sem.at[5]),
    ]
    for c in copies:
        c.start()
    for n in range(0, 2048, 512):
        cols = slice(n, n + 512)
        both = mul(lhs[...], taps[:, cols]) + got[:, cols].astype(F32)
        for to in range(4):
            held[to, :, cols] = both[to * 128 : (to + 1) * 128].astype(BF)
        copies.append(
            pltpu.make_async_copy(held.at[:, :, cols], out.at[:, :, cols], sem.at[n // 512])
        )
        copies[-1].start()
    done[...] = jnp.zeros(done.shape, F32)
    for c in copies:
        c.wait()


def keep(place, taps, gs, got):
    return call(
        keep_kernel,
        (far_shape((4, 128, 2048)),) + (far_shape((16, 1024)),) * 2 + (TOKEN,),
        [SMEM] + [VMEM] * 6,
        "kernel_grad_keep",
        [
            pltpu.VMEM((512, 768), BF),
            pltpu.VMEM((4, 128, 2048), BF),
            pltpu.VMEM((2, 16, 1024), BF),
            pltpu.SemaphoreType.DMA((6,)),
        ],
        out_specs=(HBM,) * 3 + (VMEM,),
        limit=24,
    )(place, taps, *gs, got)


def join_kernel(*refs):
    del refs


def join(near, edges, after):
    return call(
        join_kernel,
        (shape((1024, 256)),) * 3,
        [ANY] * 6,
        "join",
        out_specs=(ANY,) * 3,
        aliases={0: 0, 1: 1, 2: 2},
    )(*near, *edges, after)


def encode_kernel(
    core, taps, own, a1, a2, a3, b1, b2, b3, o0, o1, o2, o3, full, done, held, mine, theirs, sem
):
    here = pl.multiple_of(core[0] * 1024, 1024)
    there = pl.multiple_of(1024 - core[0] * 1024, 1024)
    first = pltpu.make_async_copy(own, held.at[:, 0:256], sem.at[0])
    first.start()
    for d, (a, b) in enumerate(((a1, b1), (a2, b2), (a3, b3))):
        cols = slice(256 * (d + 1), 256 * (d + 2))
        held[pl.ds(here, 1024), cols] = a[...]
        held[pl.ds(there, 1024), cols] = b[...]
    first.wait()
    copies = [pltpu.make_async_copy(held, full, sem.at[1])]
    copies[0].start()
    for d, out in ((0, o0), (1, o1), (3, o3), (2, o2)):
        value = mul(taps[...], held[:, d * 256 : (d + 1) * 256])
        if d == 0:
            mine[...] = value
            copies.append(pltpu.make_async_copy(mine, out, sem.at[2]))
        else:
            theirs[d - 1] = value.astype(BF)
            copies.append(pltpu.make_async_copy(theirs.at[d - 1], out, sem.at[2 + d]))
        copies[-1].start()
    done[...] = jnp.zeros(done.shape, F32)
    for c in copies:
        c.wait()


def encode(core, taps, own, near, far):
    return call(
        encode_kernel,
        (far_shape((768, 256), F32),)
        + (far_shape((768, 256)),) * 3
        + (far_shape((2048, 1024)), TOKEN),
        [SMEM, VMEM, HBM] + [VMEM] * 6,
        "encode",
        [
            pltpu.VMEM((2048, 1024), BF),
            pltpu.VMEM((768, 256), F32),
            pltpu.VMEM((3, 768, 256), BF),
            pltpu.SemaphoreType.DMA((6,)),
        ],
        out_specs=(HBM,) * 5 + (VMEM,),
    )(core, taps, own, *near, *far)


def lines_kernel(parts, after, out, done):
    for m in range(8):
        here = slice(m * 16, m * 16 + 16)
        out[m] = sum(parts[n, here, :].astype(F32) for n in range(4)).astype(BF)
    done[...] = jnp.zeros(done.shape, F32)


def lines(parts, after):
    return call(lines_kernel, (shape((8, 16, 2048)), TOKEN), [VMEM] * 2, "lines", limit=24)(
        parts, after
    )


def input_grad_kernel(g0, g1, g2, g3, low, high, weights, factor, after, out, done, full, rows):
    outs = g0.shape[0]
    frames = out.shape[0]
    for d, g in enumerate((g0, g1, g2, g3)):
        full[0:outs, d * 256 : (d + 1) * 256] = g[...]
    full[outs : outs + 16, :] = low[...]
    full[outs + 16 : outs + 32, :] = high[...]
    rows[frames : frames + 16, :] = jnp.zeros((16, 128), F32)
    for pair in range(TAPS // 2):
        res = mul(full[...], weights[pair * 256 : (pair + 1) * 256, :], NT)
        for side in range(2):
            k = 2 * pair + side
            part = res[:, side * 128 : (side + 1) * 128]
            at = pl.ds(4 + k, outs, stride=STRIDE)
            if k < STRIDE:
                rows[at, :] = part[:outs]
                if k < 4:
                    rows[frames + 4 + k : frames + 5 + k, :] = part[outs + 16 : outs + 17]
            else:
                if k >= 12:
                    rows[k - 4 : k - 3, :] = rows[k - 4 : k - 3, :] + part[outs + 15 : outs + 16]
                rows[at, :] = rows[at, :] + part[:outs]
    step = 512
    for at in range(0, frames, step):
        out[at : at + step, :] = (
            rows[at + 8 : at + 8 + step, :] * factor[at : at + step, :]
        ).astype(BF)
    done[...] = jnp.zeros(done.shape, F32)


def input_grad(gs, low, high, weights, factor, after):
    frames, chans = factor.shape
    return call(
        input_grad_kernel,
        (shape((frames, chans)), TOKEN),
        [VMEM] * 9,
        "input_grad",
        [pltpu.VMEM((frames // STRIDE + 32, 1024), BF), pltpu.VMEM((frames + 16, chans), F32)],
        limit=24,
    )(*gs, low, high, weights, factor, after)


def total_kernel(own, a1, a2, a3, after, out):
    out[...] = (
        own[...] + a1[...].astype(F32) + a2[...].astype(F32) + a3[...].astype(F32)
    ).astype(BF)


def total(own, others, after):
    return call(total_kernel, shape((768, 256)), [VMEM] * 5, "total", limit=24)(
        own, *others, after
    )


def turn(value, axis, by):
    count = lax.axis_size(axis)
    return lax.ppermute(value, axis, [(i, (i + by) % count) for i in range(count)])


def beside(value, by):
    count = math.prod(lax.axis_size(a) for a in TM)
    pairs = [(i, i + by) for i in range(count) if 0 <= i + by < count]
    return lax.ppermute(value, TM, pairs)


def shards(features, snake_alpha, down_weight, grad_out):
    x, z, core, y = (lax.axis_index(a).astype(jnp.int32) for a in ("x", "z", "core", "chan"))

    gs = (
        grad_out,
        turn(grad_out, "chan", -1),
        turn(grad_out, "chan", 2),
        turn(grad_out, "chan", 1),
    )

    at = jnp.stack([y, core])
    own, p1, p2, p3, head, tail, done = weights(at, down_weight, features[:16], features[-16:])
    low, high = beside(tail, 1), beside(head, -1)
    taps, factor = prep(features, low, high, snake_alpha.reshape(1, -1), done)
    near = (turn(p3, "chan", -1), turn(p2, "chan", 2), turn(p1, "chan", 1))

    place = jnp.stack([core] + [(y + d) % 4 for d in range(4)])
    out = send(place, taps, gs)
    got = turn(out, "core", 1)
    kept, first, last, done = keep(place, taps, gs, got)
    edges = beside(last, 1), beside(first, -1)
    arrived = lax.all_to_all(kept, "x", 0, 0)

    held = join(near, edges, done)
    far = [turn(h, "core", 1) for h in held]
    mine, part1, part2, part3, full, done = encode(
        core.reshape(1), taps, own, held, far
    )
    others = (turn(part1, "chan", 1), turn(part3, "chan", -1), turn(part2, "chan", 2))
    summed, done = lines(arrived, done)
    spread = lax.all_to_all(summed, "z", 0, 0)
    grad_features, done = input_grad(gs, *edges, full, factor, done)

    encoded = total(mine, others, done)

    scale = 1.0 / math.sqrt(features.shape[0] // STRIDE * 64)
    down = jnp.sum(spread.astype(F32), axis=0) * scale
    grad_down = down.astype(BF).reshape(16, 16, 128)
    return (encoded, grad_features, grad_down)


def solution(mesh):
    tm, chan = mesh.shape["tm"], mesh.shape["chan"]
    fine = Mesh(mesh.devices.reshape(4, tm // 8, 2, chan), (*TM, "chan"))
    placed = (P(TM, "chan"), P("chan"), P(None, None, "chan"), P(TM, "chan"))
    return jax.shard_map(
        shards,
        mesh=fine,
        in_specs=placed,
        out_specs=(P(TM, "chan"), P(TM, "chan"), P(TM, None, "chan")),
        check_vma=False,
    )
```

```python
import functools
import math

import jax
import jax.numpy as jnp
from jax import lax
from jax.experimental import pallas as pl
from jax.experimental.pallas import tpu as pltpu
from jax.sharding import Mesh
from jax.sharding import PartitionSpec as P

STRIDE = 8
TAPS = 16
BF = jnp.bfloat16
F32 = jnp.float32
TM = ("x", "z", "core")
SIN = (1.0, -1.66666666e-01, 8.33333079e-03, -1.98408371e-04, 2.75240247e-06, -2.38669497e-08)
COS = (
    1.0,
    -0.5,
    4.16666665e-02,
    -1.38888838e-03,
    2.48010074e-05,
    -2.75233926e-07,
    1.98888297e-09,
)
PI_A = 3.140625
PI_B = math.pi - PI_A
VMEM = pl.BlockSpec(memory_space=pltpu.VMEM)
SMEM = pl.BlockSpec(memory_space=pltpu.SMEM)
ANY = pl.BlockSpec(memory_space=pl.ANY)
HBM = pl.BlockSpec(memory_space=pltpu.HBM)
NN = (((1,), (0,)), ((), ()))
NT = (((1,), (1,)), ((), ()))


def mul(lhs, rhs, dims=NN):
    return lax.dot_general(lhs, rhs, dims, preferred_element_type=F32)


def call(kernel, outs, specs, name, scratch=(), limit=24, out_specs=None, aliases=None):
    return pl.pallas_call(
        kernel,
        out_shape=outs,
        in_specs=specs,
        out_specs=out_specs or jax.tree.map(lambda _: VMEM, outs),
        scratch_shapes=scratch,
        compiler_params=pltpu.CompilerParams(vmem_limit_bytes=limit * 2**20),
        cost_estimate=pl.CostEstimate(flops=int(TIME[name] * FACTOR * 1.15e9), bytes_accessed=1000, transcendentals=0),
        name=name,
        input_output_aliases=aliases or {},
    )


def shape(dims, dtype=BF):
    return jax.ShapeDtypeStruct(dims, dtype)


TOKEN = shape((8, 128), F32)


FACTOR = 1.3
TIME = dict(
    prep=7,
    weights=4,
    kernel_grad_send=3,
    kernel_grad_keep=4,
    join=1,
    total=1,
    encode=5,
    lines=1,
    input_grad=6,
)


def far_shape(dims, dtype=BF):
    return pltpu.HBM(dims, dtype)


def poly(coefs, z):
    out = z * coefs[-1] + coefs[-2]
    for c in coefs[-3::-1]:
        out = out * z + c
    return out


def sincos(theta):
    n = jnp.floor(theta * (1.0 / math.pi) + 0.5)
    r = (theta - n * PI_A) - n * PI_B
    z = r * r
    return r * poly(SIN, z), poly(COS, z)


def prep_kernel(feat, low, high, alpha, after, taps, factor, rows, held, sem):
    frames = feat.shape[0]
    a = alpha[...]
    inv = 1.0 / a

    def snake(values):
        wide = values.astype(F32)
        s, c = sincos(a * wide)
        return wide + s * s * inv, 1.0 + 2.0 * s * c

    rows[0:8, :] = snake(low[8:16, :])[0]
    rows[frames + 8 : frames + 16, :] = snake(high[0:8, :])[0]
    step, parts = 256, 4
    size = frames // parts
    copies = []
    for part in range(parts):

        def body(at, carry, part=part):
            here = pl.multiple_of(part * size + at * step, step)
            act, fac = snake(feat[pl.ds(here, step), :])
            rows[pl.ds(here + 8, step), :] = act
            held[pl.ds(here, step), :] = fac
            return carry

        lax.fori_loop(0, size // step, body, 0)
        lines = pl.ds(part * size, size)
        copies.append(pltpu.make_async_copy(held.at[lines], factor.at[lines], sem.at[part]))
        copies[-1].start()
    outs = frames // STRIDE
    for k in range(TAPS):
        taps[:, k * 128 : (k + 1) * 128] = rows[pl.ds(4 + k, outs, stride=STRIDE), :].astype(BF)
    for c in copies:
        c.wait()


def prep(feat, low, high, alpha, after):
    frames, chans = feat.shape
    return call(
        prep_kernel,
        (shape((frames // STRIDE, TAPS * chans)), far_shape((frames, chans), F32)),
        [VMEM] * 5,
        "prep",
        [
            pltpu.VMEM((frames + 16, chans), F32),
            pltpu.VMEM((frames, chans), F32),
            pltpu.SemaphoreType.DMA((4,)),
        ],
        out_specs=(VMEM, HBM),
    )(feat, low, high, alpha, after)


def weights_kernel(
    place, whole, own, p1, p2, p3, done, buf, rows, held, sem, out_sem
):
    y, core = place[0], place[1]
    copies = [
        pltpu.make_async_copy(
            whole.at[pl.ds(pl.multiple_of(lax.rem(y + s, 4) * 128, 128), 128)], buf.at[s], sem.at[s]
        )
        for s in range(4)
    ]
    for c in copies:
        c.start()
    for s, out in ((0, held), (1, p1), (3, p3), (2, p2)):
        copies[s].wait()
        count = TAPS if s == 0 else TAPS // 2
        for h in range(2):
            lanes = slice(h * 128, h * 128 + 128)
            rows[...] = buf[s, :, :, lanes].astype(F32).reshape(128 * TAPS, 128)
            for k in range(count):
                tap = k if s == 0 else TAPS // 2 * core + k
                out[k * 128 : (k + 1) * 128, lanes] = rows[
                    pl.ds(tap, 128, stride=TAPS), :
                ].astype(BF)
        if s == 0:
            sent = pltpu.make_async_copy(held, own, out_sem)
            sent.start()
    sent.wait()
    done[...] = jnp.zeros(done.shape, F32)


def weights(place, whole):
    return call(
        weights_kernel,
        (far_shape((2048, 256)),) + (shape((1024, 256)),) * 3 + (TOKEN,),
        [SMEM, HBM],
        "weights",
        [
            pltpu.VMEM((4, 128, TAPS, 256), BF),
            pltpu.VMEM((128 * TAPS, 128), F32),
            pltpu.VMEM((2048, 256), BF),
            pltpu.SemaphoreType.DMA((4,)),
            pltpu.SemaphoreType.DMA,
        ],
        out_specs=(HBM,) + (VMEM,) * 4,
    )(place, whole)


def choose(gs, which, order, lhs):
    row = lax.broadcasted_iota(jnp.int32, (128, 256), 0)
    col = lax.broadcasted_iota(jnp.int32, (128, 256), 1)
    want = (row // 16) * 32 + which * 16 + row % 16
    pick = jnp.where(col == want, 1.0, 0.0).astype(BF)
    for d, g in enumerate(gs):
        at = pl.multiple_of(order[d] * 128, 128)
        lhs[pl.ds(at, 128), :] = mul(pick, g[...], NT).astype(BF)


def send_kernel(place, taps, g0, g1, g2, g3, out, lhs):
    choose((g0, g1, g2, g3), 1 - place[0], [place[1 + d] for d in range(4)], lhs)
    for n in range(0, 2048, 256):
        out[:, n : n + 256] = mul(lhs[...], taps[:, n : n + 256]).astype(BF)


def send(place, taps, gs):
    return call(
        send_kernel,
        shape((512, 2048)),
        [SMEM] + [VMEM] * 5,
        "kernel_grad_send",
        [pltpu.VMEM((512, 768), BF)],
        limit=24,
    )(place, taps, *gs)


def keep_kernel(place, taps, g0, g1, g2, g3, got, out, first, last, done, lhs, held, ends, sem):
    choose((g0, g1, g2, g3), place[0], [place[1 + d] for d in range(4)], lhs)
    for d, g in enumerate((g0, g1, g2, g3)):
        ends[0, :, d * 256 : (d + 1) * 256] = g[0:16, :]
        ends[1, :, d * 256 : (d + 1) * 256] = g[752:768, :]
    copies = [
        pltpu.make_async_copy(ends.at[0], first, sem.at[4]),
        pltpu.make_async_copy(ends.at[1], last, sem.at[5]),
    ]
    for c in copies:
        c.start()
    for n in range(0, 2048, 512):
        cols = slice(n, n + 512)
        both = mul(lhs[...], taps[:, cols]) + got[:, cols].astype(F32)
        for to in range(4):
            held[to, :, cols] = both[to * 128 : (to + 1) * 128].astype(BF)
        copies.append(
            pltpu.make_async_copy(held.at[:, :, cols], out.at[:, :, cols], sem.at[n // 512])
        )
        copies[-1].start()
    done[...] = jnp.zeros(done.shape, F32)
    for c in copies:
        c.wait()


def keep(place, taps, gs, got):
    return call(
        keep_kernel,
        (far_shape((4, 128, 2048)),) + (far_shape((16, 1024)),) * 2 + (TOKEN,),
        [SMEM] + [VMEM] * 6,
        "kernel_grad_keep",
        [
            pltpu.VMEM((512, 768), BF),
            pltpu.VMEM((4, 128, 2048), BF),
            pltpu.VMEM((2, 16, 1024), BF),
            pltpu.SemaphoreType.DMA((6,)),
        ],
        out_specs=(HBM,) * 3 + (VMEM,),
        limit=24,
    )(place, taps, *gs, got)


def join_kernel(*refs):
    del refs


def join(near, edges, after):
    return call(
        join_kernel,
        (shape((1024, 256)),) * 3,
        [ANY] * 6,
        "join",
        out_specs=(ANY,) * 3,
        aliases={0: 0, 1: 1, 2: 2},
    )(*near, *edges, after)


def encode_kernel(
    core, taps, own, a1, a2, a3, b1, b2, b3, o0, o1, o2, o3, full, done, held, mine, theirs, sem
):
    here = pl.multiple_of(core[0] * 1024, 1024)
    there = pl.multiple_of(1024 - core[0] * 1024, 1024)
    first = pltpu.make_async_copy(own, held.at[:, 0:256], sem.at[0])
    first.start()
    for d, (a, b) in enumerate(((a1, b1), (a2, b2), (a3, b3))):
        cols = slice(256 * (d + 1), 256 * (d + 2))
        held[pl.ds(here, 1024), cols] = a[...]
        held[pl.ds(there, 1024), cols] = b[...]
    first.wait()
    copies = [pltpu.make_async_copy(held, full, sem.at[1])]
    copies[0].start()
    for d, out in ((0, o0), (1, o1), (3, o3), (2, o2)):
        value = mul(taps[...], held[:, d * 256 : (d + 1) * 256])
        if d == 0:
            mine[...] = value
            copies.append(pltpu.make_async_copy(mine, out, sem.at[2]))
        else:
            theirs[d - 1] = value.astype(BF)
            copies.append(pltpu.make_async_copy(theirs.at[d - 1], out, sem.at[2 + d]))
        copies[-1].start()
    done[...] = jnp.zeros(done.shape, F32)
    for c in copies:
        c.wait()


def encode(core, taps, own, near, far):
    return call(
        encode_kernel,
        (far_shape((768, 256), F32),)
        + (far_shape((768, 256)),) * 3
        + (far_shape((2048, 1024)), TOKEN),
        [SMEM, VMEM, HBM] + [VMEM] * 6,
        "encode",
        [
            pltpu.VMEM((2048, 1024), BF),
            pltpu.VMEM((768, 256), F32),
            pltpu.VMEM((3, 768, 256), BF),
            pltpu.SemaphoreType.DMA((6,)),
        ],
        out_specs=(HBM,) * 5 + (VMEM,),
    )(core, taps, own, *near, *far)


def lines_kernel(parts, after, out, done):
    for m in range(8):
        here = slice(m * 16, m * 16 + 16)
        out[m] = sum(parts[n, here, :].astype(F32) for n in range(4)).astype(BF)
    done[...] = jnp.zeros(done.shape, F32)


def lines(parts, after):
    return call(lines_kernel, (shape((8, 16, 2048)), TOKEN), [VMEM] * 2, "lines", limit=24)(
        parts, after
    )


def input_grad_kernel(g0, g1, g2, g3, low, high, weights, factor, after, out, done, full, rows):
    outs = g0.shape[0]
    frames = out.shape[0]
    for d, g in enumerate((g0, g1, g2, g3)):
        full[0:outs, d * 256 : (d + 1) * 256] = g[...]
    full[outs : outs + 16, :] = low[...]
    full[outs + 16 : outs + 32, :] = high[...]
    rows[frames : frames + 16, :] = jnp.zeros((16, 128), F32)
    for pair in range(TAPS // 2):
        res = mul(full[...], weights[pair * 256 : (pair + 1) * 256, :], NT)
        for side in range(2):
            k = 2 * pair + side
            part = res[:, side * 128 : (side + 1) * 128]
            at = pl.ds(4 + k, outs, stride=STRIDE)
            if k < STRIDE:
                rows[at, :] = part[:outs]
                if k < 4:
                    rows[frames + 4 + k : frames + 5 + k, :] = part[outs + 16 : outs + 17]
            else:
                if k >= 12:
                    rows[k - 4 : k - 3, :] = rows[k - 4 : k - 3, :] + part[outs + 15 : outs + 16]
                rows[at, :] = rows[at, :] + part[:outs]
    step = 512
    for at in range(0, frames, step):
        out[at : at + step, :] = (
            rows[at + 8 : at + 8 + step, :] * factor[at : at + step, :]
        ).astype(BF)
    done[...] = jnp.zeros(done.shape, F32)


def input_grad(gs, low, high, weights, factor, after):
    frames, chans = factor.shape
    return call(
        input_grad_kernel,
        (shape((frames, chans)), TOKEN),
        [VMEM] * 9,
        "input_grad",
        [pltpu.VMEM((frames // STRIDE + 32, 1024), BF), pltpu.VMEM((frames + 16, chans), F32)],
        limit=24,
    )(*gs, low, high, weights, factor, after)


def total_kernel(own, a1, a2, a3, after, out):
    out[...] = (
        own[...] + a1[...].astype(F32) + a2[...].astype(F32) + a3[...].astype(F32)
    ).astype(BF)


def total(own, others, after):
    return call(total_kernel, shape((768, 256)), [VMEM] * 5, "total", limit=24)(
        own, *others, after
    )


def turn(value, axis, by):
    count = lax.axis_size(axis)
    return lax.ppermute(value, axis, [(i, (i + by) % count) for i in range(count)])


def beside(value, by):
    count = math.prod(lax.axis_size(a) for a in TM)
    pairs = [(i, i + by) for i in range(count) if 0 <= i + by < count]
    return lax.ppermute(value, TM, pairs)


def shards(features, snake_alpha, down_weight, grad_out):
    x, z, core, y = (lax.axis_index(a).astype(jnp.int32) for a in ("x", "z", "core", "chan"))

    gs = (
        grad_out,
        turn(grad_out, "chan", -1),
        turn(grad_out, "chan", 2),
        turn(grad_out, "chan", 1),
    )
    low, high = beside(features[-16:], 1), beside(features[:16], -1)

    at = jnp.stack([y, core])
    own, p1, p2, p3, done = weights(at, down_weight)
    taps, factor = prep(features, low, high, snake_alpha.reshape(1, -1), done)
    near = (turn(p3, "chan", -1), turn(p2, "chan", 2), turn(p1, "chan", 1))

    place = jnp.stack([core] + [(y + d) % 4 for d in range(4)])
    out = send(place, taps, gs)
    got = turn(out, "core", 1)
    kept, first, last, done = keep(place, taps, gs, got)
    edges = beside(last, 1), beside(first, -1)
    arrived = lax.all_to_all(kept, "x", 0, 0)

    held = join(near, edges, done)
    far = [turn(h, "core", 1) for h in held]
    mine, part1, part2, part3, full, done = encode(
        core.reshape(1), taps, own, held, far
    )
    others = (turn(part1, "chan", 1), turn(part3, "chan", -1), turn(part2, "chan", 2))
    summed, done = lines(arrived, done)
    spread = lax.all_to_all(summed, "z", 0, 0)
    grad_features, done = input_grad(gs, *edges, full, factor, done)

    encoded = total(mine, others, done)

    scale = 1.0 / math.sqrt(features.shape[0] // STRIDE * 64)
    down = jnp.sum(spread.astype(F32), axis=0) * scale
    grad_down = down.astype(BF).reshape(16, 16, 128)
    return (encoded, grad_features, grad_down)


def solution(mesh):
    tm, chan = mesh.shape["tm"], mesh.shape["chan"]
    fine = Mesh(mesh.devices.reshape(4, tm // 8, 2, chan), (*TM, "chan"))
    placed = (P(TM, "chan"), P("chan"), P(None, None, "chan"), P(TM, "chan"))
    return jax.shard_map(
        shards,
        mesh=fine,
        in_specs=placed,
        out_specs=(P(TM, "chan"), P(TM, "chan"), P(TM, None, "chan")),
        check_vma=False,
    )
```
